32 devices in a mesh: parts: 2 (over x), tm: 16 (over z, y, core).
Axes of the slice: x: 2, y: 2, z: 4, core: 2. Of those that a mesh axis runs over, the one named last changes fastest.
Arguments:
- observed: float32 [64, 128], P(('parts', 'tm')), parts along dimension 0, may hold values from -6 to 6
- obs_mask: int32 [64, 128], P(('parts', 'tm')), parts along dimension 0, may hold values 0 or 1
- prior_mean: float32 [256], P('parts'), parts along dimension 0, may hold values from -6 to 6
- prior_var: float32 [256], P('parts'), parts along dimension 0, may hold values from 0.5 to 2
- neighbor_weights: float32 [8, 128], replicated, may hold values from 0.01 to 0.06
- damping: float32 [128], replicated, may hold values from 0.0005 to 0.005
- process_var: float32 [128], replicated, may hold values from 0.0005 to 0.002
- obs_var: float32 [128], replicated, may hold values from 1 to 4
Outputs:
- smoothed_mean: float32 [64, 128], P(('parts', 'tm')), parts along dimension 0
- smoothed_cov: float32 [64, 128, 128], P(('parts', 'tm')), parts along dimension 0
- loglik: float32 [64], P(('parts', 'tm')), parts along dimension 0
The draws below stay inside these ranges and needn't reach their ends.
There are 2 independent parts, one for each index of `parts`. The reference program is written for one: setup_inputs(seed, part) draws one part's arguments, and reference() takes and returns one part's arrays. A program takes and returns all parts, laid end to end along the dimension named above; an argument that names none is the same for every part. Nothing has to cross between parts.
Inputs may be any that keep to these rules, and one draw needn't show every extreme that they name: `obs_mask`: 1 where a cell is observed at a step, 0 where it is not.
All inputs are finite; a program needn't handle non-finite values. No bound on the sum of `obs_mask` on one device may be relied on, other than what follows from the above.
Results may differ from the reference program's by a relative error of at most 0.0003.
Values sent between devices are 32-bit elements; how exact they have to be, the bound alone decides.
No kernel may reach another device: no remote copies, remote signals or barrier semaphores. Data moves between devices by JAX's collectives and lax.ppermute only.
A program may use at most 128 MiB of HBM per device.

```python
import math
import jax
import jax.numpy as jnp
from jax import lax

GX = 16
GY = 8
NS = 128
STEPS = 32


def with_ends(result, rng, smallest, largest):
    dims = result.shape
    spot = [jax.random.randint(jax.random.fold_in(rng, axis), (), 0, dims[axis]) for axis in range(len(dims))]
    result = result.at[tuple(spot)].set(smallest)
    longest = dims.index(max(dims))
    spot[longest] = (spot[longest] + 1) % dims[longest]
    return result.at[tuple(spot)].set(largest)


def levels(rng, dims, pieces, smallest, top_value):
    factor_of = 1.0
    for position, blocks in pieces:
        draws = jax.random.uniform(jax.random.fold_in(jax.random.fold_in(rng, 6), position), (blocks,), jnp.float32, smallest / len(pieces), top_value / len(pieces))
        factor_of = factor_of * jnp.repeat(jnp.exp(draws), dims[position] // blocks).reshape((-1,) + (1,) * (len(dims) - 1 - position))
    return factor_of


def gaussian(own_key, extent, spread, reach, cuts=(), dtype=jnp.bfloat16):
    level = levels(own_key, extent, cuts, -0.22, 0.18) if cuts else 1.0
    result = jax.random.normal(own_key, extent, jnp.float32) * spread * level
    return jnp.minimum(jnp.maximum(result, -reach), reach).astype(dtype)


def setup_inputs(seed: int = 0, part: int = 0) -> dict:
    arg_keys = jax.random.split(jax.random.key(seed), 9)
    part_splits = jax.random.split(jax.random.fold_in(arg_keys[8], part), 9)
    observed = gaussian(part_splits[0], (STEPS, NS), 1.0, 6.0, ((0, 16),), jnp.float32)
    obs_mask = with_ends((jax.random.randint(part_splits[1], (STEPS, NS), 0, 16) < 1).astype(jnp.int32), jax.random.fold_in(part_splits[1], 1), 0, 1)
    prior_mean = gaussian(part_splits[2], (NS,), 1.0, 6.0, (), jnp.float32)
    prior_var = jnp.clip(jnp.exp(jax.random.uniform(part_splits[3], (NS,), jnp.float32, math.log(0.5), math.log(2.0))), 0.5, 2.0)
    neighbor_weights = jnp.clip(jax.random.uniform(arg_keys[4], (8, NS), jnp.float32, 0.01, 0.06), 0.01, 0.06)
    damping = jnp.clip(jnp.exp(jax.random.uniform(arg_keys[5], (NS,), jnp.float32, math.log(0.0005), math.log(0.005))), 0.0005, 0.005)
    process_var = jnp.clip(jnp.exp(jax.random.uniform(arg_keys[6], (NS,), jnp.float32, math.log(0.0005), math.log(0.002))), 0.0005, 0.002)
    obs_var = jnp.clip(jnp.exp(jax.random.uniform(arg_keys[7], (NS,), jnp.float32, math.log(1.0), math.log(4.0))), 1.0, 4.0)
    return {"observed": observed, "obs_mask": obs_mask, "prior_mean": prior_mean, "prior_var": prior_var, "neighbor_weights": neighbor_weights, "damping": damping, "process_var": process_var, "obs_var": obs_var}


OFFSETS = ((-1, -1), (-1, 0), (-1, 1), (0, -1), (0, 1), (1, -1), (1, 0), (1, 1))
LOG_TWO_PI = math.log(2.0 * math.pi)

def high_dot(left, right):
    return jnp.dot(left.astype(jnp.float32), right.astype(jnp.float32), precision=lax.Precision.HIGHEST, preferred_element_type=jnp.float32)

def advance(matrix_in, neighbor_weights, damping):
    centre = 1.0 - jnp.sum(neighbor_weights, axis=0) - damping
    columns = matrix_in.shape[1]
    gridded = matrix_in.reshape(GX, GY, columns)
    padded = jnp.pad(gridded, ((1, 1), (1, 1), (0, 0)))
    summed = centre.reshape(GX, GY, 1) * gridded
    for offset_index in range(8):
        shift_x, shift_y = OFFSETS[offset_index]
        summed = summed + neighbor_weights[offset_index].reshape(GX, GY, 1) * padded[1 + shift_x:1 + shift_x + GX, 1 + shift_y:1 + shift_y + GY]
    return summed.reshape(GX * GY, columns)

def predict(mean_in, cov_in, neighbor_weights, damping, process_var):
    pred_mean = advance(mean_in[:, None], neighbor_weights, damping)[:, 0]
    moved_cov = advance(cov_in, neighbor_weights, damping)
    pred_cov = advance(moved_cov.T, neighbor_weights, damping).T + jnp.diag(process_var)
    return (pred_mean, pred_cov)

def update(pred_mean, pred_cov, obs_row, mask_row, obs_var):
    mask_val = mask_row.astype(jnp.float32)
    masked = mask_val[:, None] * pred_cov
    innov_cov = masked * mask_val[None, :] + jnp.diag(obs_var)
    chol_s = jnp.linalg.cholesky(innov_cov)
    innov = mask_val * (obs_row - pred_mean)
    solved = jax.scipy.linalg.cho_solve((chol_s, True), innov)
    rhs_mat = jax.scipy.linalg.cho_solve((chol_s, True), masked)
    new_mean = pred_mean + high_dot(masked.T, solved)
    new_cov = pred_cov - high_dot(masked.T, rhs_mat)
    whitened = jax.scipy.linalg.solve_triangular(chol_s, innov, lower=True)
    logdet = 2.0 * jnp.sum(jnp.log(jnp.diagonal(chol_s)))
    density = -(logdet - jnp.sum((1.0 - mask_val) * jnp.log(obs_var)) + jnp.sum(whitened * whitened) + jnp.sum(mask_val) * LOG_TWO_PI) / (2.0 * NS)
    return (new_mean, new_cov, density)

def reference(observed, obs_mask, prior_mean, prior_var, neighbor_weights, damping, process_var, obs_var):
    first_mean, first_cov, first_density = update(prior_mean, jnp.diag(prior_var), observed[0], obs_mask[0], obs_var)

    def forward(state_in, inputs):
        mean_in, cov_in = state_in
        obs_row, mask_row = inputs
        pred_mean, pred_cov = predict(mean_in, cov_in, neighbor_weights, damping, process_var)
        new_mean, new_cov, density = update(pred_mean, pred_cov, obs_row, mask_row, obs_var)
        return ((new_mean, new_cov), (new_mean, new_cov, density))
    unused, (means, covs, densities) = lax.scan(forward, (first_mean, first_cov), (observed[1:], obs_mask[1:]))
    means = jnp.concatenate([first_mean[None], means], axis=0)
    covs = jnp.concatenate([first_cov[None], covs], axis=0)
    densities = jnp.concatenate([first_density[None], densities], axis=0)

    def backward(state_in, inputs):
        smooth_mean, smooth_cov = state_in
        mean_in, cov_in = inputs
        moved_cov = advance(cov_in, neighbor_weights, damping)
        pred_cov = advance(moved_cov.T, neighbor_weights, damping).T + jnp.diag(process_var)
        pred_mean = advance(mean_in[:, None], neighbor_weights, damping)[:, 0]
        chol_p = jnp.linalg.cholesky(pred_cov)
        gain_t = jax.scipy.linalg.cho_solve((chol_p, True), moved_cov)
        gain = gain_t.T
        new_mean = mean_in + high_dot(gain, smooth_mean - pred_mean)
        new_cov = cov_in + high_dot(gain, high_dot(smooth_cov - pred_cov, gain_t))
        return ((new_mean, new_cov), (new_mean, new_cov))
    unused_two, (smooth_means, smooth_covs) = lax.scan(backward, (means[-1], covs[-1]), (means[:-1], covs[:-1]), reverse=True)
    smoothed_mean = jnp.concatenate([smooth_means, means[-1:]], axis=0)
    smoothed_cov = jnp.concatenate([smooth_covs, covs[-1:]], axis=0)
    return (smoothed_mean, smoothed_cov, densities)
```

```python
import functools
import math

import jax
import jax.numpy as jnp
from jax import lax
from jax.experimental import pallas as pl
from jax.experimental.pallas import tpu as pltpu
from jax.sharding import PartitionSpec as P

GX = 16
GY = 8
OFFSETS = ((-1, -1), (-1, 0), (-1, 1), (0, -1), (0, 1), (1, -1), (1, 0), (1, 1))
LOG_TWO_PI = math.log(2.0 * math.pi)

WINDOW = 4
SLOTS = 48
FAR = 1 << 29

NN = (((1,), (0,)), ((), ()))
NT = (((1,), (1,)), ((), ()))
TN = (((0,), (0,)), ((), ()))
BF = jnp.bfloat16
F32 = jnp.float32


def halves(x):
    high = x.astype(BF)
    return high, (x - high.astype(F32)).astype(BF)


def as_left(x, axis):
    high, low = halves(x)
    return jnp.concatenate([high, high, low], axis=axis)


def as_right(x, axis):
    high, low = halves(x)
    return jnp.concatenate([high, low, high], axis=axis)


def raw(left, right, dims):
    return lax.dot_general(left, right, dims, preferred_element_type=F32)


def dot(left, right, dims=NN):
    (left_axis,), (right_axis,) = dims[0]
    return raw(as_left(left, left_axis), as_right(right, right_axis), dims)


def exact_dot(ones_left, right, dims=NN):
    (left_axis,), (right_axis,) = dims[0]
    high, low = halves(right)
    left = ones_left.astype(BF)
    return raw(
        jnp.concatenate([left, left], axis=left_axis),
        jnp.concatenate([high, low], axis=right_axis),
        dims,
    )


def iota(shape, axis):
    return lax.broadcasted_iota(jnp.int32, shape, axis)


def transition(nw, damping):
    size = GX * GY
    source, cell = iota((size, size), 0), iota((size, size), 1)
    row, column = cell // GY, cell % GY
    source_row, source_column = source // GY, source % GY
    centre = 1.0 - jnp.sum(nw, axis=0, keepdims=True) - damping
    flipped = jnp.where(source == cell, centre, 0.0)
    for index, (dx, dy) in enumerate(OFFSETS):
        hit = (source_row == row + dx) & (source_column == column + dy)
        flipped = flipped + jnp.where(hit, nw[index : index + 1, :], 0.0)
    return jnp.transpose(flipped)


def eliminate(square, sides):
    tiles = SLOTS // 8
    rows = iota((8, 128), 0)
    columns = {}
    for k in range(SLOTS - 1):
        for tile in range(k // 8, tiles):
            block = square[8 * tile : 8 * tile + 8, k : k + 1]
            columns[k, tile] = jnp.broadcast_to(block, (8, 128))
    parts = [[side[8 * t : 8 * t + 8, :] for t in range(tiles)] for side in sides]
    pivots = [jnp.ones((8, 128), F32) for _ in range(tiles)]
    quad = jnp.zeros((8, 128), F32)

    def spread(block, row):
        return jnp.broadcast_to(block[row : row + 1, :], (8, 128))

    for j in range(SLOTS - 1):
        home, row = divmod(j, 8)
        pivot = spread(columns[j, home], row)
        pivots[home] = jnp.where(rows == row, pivot, pivots[home])
        inverse = 1.0 / pivot
        weights = {}
        for tile in range(home, tiles):
            scaled = columns[j, tile] * inverse
            if tile == home:
                scaled = jnp.where(rows > row, scaled, 0.0)
            weights[tile] = scaled
        quad = quad + weights[tiles - 1] * columns[j, tiles - 1]
        for k in range(j + 1, SLOTS - 1):
            across = spread(columns[k, k // 8], row) if k // 8 == home else None
            if across is None:
                across = spread(columns[j, k // 8], k % 8)
            for tile in range(k // 8, tiles):
                columns[k, tile] = columns[k, tile] - weights[tile] * across
        for part in parts:
            across = spread(part[home], row)
            for tile in range(home, tiles):
                part[tile] = part[tile] - weights[tile] * across
    pivots = jnp.concatenate(pivots, axis=0)
    sides = [jnp.concatenate(part, axis=0) for part in parts]
    return sides, pivots, quad[7:8, :]


def chain_kernel(
    own,
    position_ref,
    gathered_ref,
    mean_ref,
    var_ref,
    nw_ref,
    damping_ref,
    process_ref,
    noise_ref,
    smooth_mean_ref,
    smooth_cov_ref,
    loglik_ref,
    mask_s,
    obs_s,
    rank_s,
    off_v,
    off_s,
    power_s,
    left_s,
    right_s,
    big_s,
    psi_s,
    added_s,
    cov_s,
    trans_s,
    info_s,
    mean_s,
    pull_s,
    kept_cov,
    kept_mean,
    kept_trans,
    kept_info,
    kept_pull,
    kept_lik,
    sem,
):
    size = GX * GY
    steps = gathered_ref.shape[0]
    padded = mask_s.shape[0]
    position = position_ref[0]
    base = position * own
    nw, damping = nw_ref[...], damping_ref[...]
    process, noise = process_ref[...], noise_ref[...]

    mask_s[...] = jnp.zeros_like(mask_s)
    obs_s[...] = jnp.zeros_like(obs_s)
    for block in range(steps // own):
        held = (position_ref[1] ^ block) * own
        for row in range(own):
            at = block * own + row
            line = gathered_ref[pl.ds(held + row, 1), :]
            obs_s[at : at + 1, :] = line[:, :size]
            mask_s[at : at + 1, :] = line[:, size:]
    mask = mask_s[...]
    mask_b = mask.astype(BF)
    before = (iota((padded, padded), 0) < iota((padded, padded), 1)).astype(BF)
    after = (iota((padded, padded), 0) > iota((padded, padded), 1)).astype(BF)
    counts_row = raw(jnp.ones((8, size), BF), mask_b, NT)
    off_v[...] = raw(counts_row.astype(BF), before, NN).astype(jnp.int32)
    copy = pltpu.make_async_copy(off_v, off_s, sem)
    copy.start()
    counts = raw(mask_b, jnp.ones((size, size), BF), NN)
    within = (iota((size, size), 0) < iota((size, size), 1)).astype(BF)
    rank = raw(mask_b, within, NN) + raw(after, counts.astype(BF), NN)
    rank_s[...] = jnp.where(mask > 0.0, rank.astype(jnp.int32), FAR)

    eye = (iota((size, size), 0) == iota((size, size), 1)).astype(F32)
    power_s[0] = eye
    power_s[1] = transition(nw, damping)
    for e in range(2, WINDOW + 1):
        power_s[e] = dot(power_s[(e + 1) // 2], power_s[e // 2])
    psi_s[...] = jnp.zeros_like(psi_s)
    big_s[...] = jnp.zeros_like(big_s)
    added_s[0] = jnp.zeros((size, size), F32)
    wide = (WINDOW - 1) * size
    for e in range(WINDOW + 1):
        left_s[e] = as_left(power_s[e], 1)
        right_s[e] = as_right(power_s[e], 1)
        if e >= 1:
            moved = power_s[e - 1]
            added_s[e] = added_s[e - 1] + dot(moved * process, moved, NT)
        for l in range(1, min(e, WINDOW - 1) + 1):
            high, low = halves(power_s[e - l])
            for piece, held in enumerate((high, low, high)):
                psi_s[e, :, piece * wide + (l - 1) * size : piece * wide + l * size] = held
    for i in range(1, WINDOW):
        for l in range(0, i):
            high, low = halves(power_s[i - l])
            for piece, held in enumerate((high, low)):
                start = piece * wide + (i - 1) * size
                big_s[start : start + size, l * size : (l + 1) * size] = held

    cov_s[...] = eye * var_ref[...]
    mean_s[...] = mean_ref[...]
    trans_s[...] = jnp.zeros_like(trans_s)
    info_s[...] = jnp.zeros_like(info_s)
    pull_s[...] = jnp.zeros_like(pull_s)
    kept_lik[...] = jnp.zeros_like(kept_lik)
    copy.wait()
    last_row = iota((SLOTS, 1), 0) == SLOTS - 1

    def body(state):
        step, first = state
        inside = (step >= base) & (step < base + own)
        cut = jnp.where(step < base, base, jnp.where(inside, step + 1, steps))
        end = jnp.minimum(step + WINDOW, cut)
        taken = jnp.minimum(off_s[0, end] - first, SLOTS - 1)
        ahead = jnp.int32(0)
        for i in range(1, WINDOW + 1):
            done = (step + i <= end) & (off_s[0, step + i] <= first + taken)
            ahead = ahead + done.astype(jnp.int32)
        mine = jnp.clip(step - base, 0, own - 1)

        @pl.when(inside & (first == off_s[0, step]))
        def _():
            kept_cov[mine] = cov_s[...]
            kept_mean[mine] = mean_s[...]
            kept_trans[mine] = trans_s[...]
            kept_info[mine] = info_s[...]
            kept_pull[mine] = pull_s[...]
            trans_s[...] = eye
            info_s[...] = jnp.zeros_like(info_s)
            pull_s[...] = jnp.zeros_like(pull_s)

        slot = iota((SLOTS, size), 0)
        picks = []
        for i in range(WINDOW):
            where = rank_s[pl.ds(step + i, 1), :] - first
            picks.append(jnp.where((slot == where) & (slot < taken), 1.0, 0.0))
        tail = jnp.concatenate(picks[1:], axis=1).astype(BF)
        spread_out = raw(jnp.concatenate([tail, tail], axis=1), big_s[...], NN)
        watch = picks[0] + spread_out[:, :size]
        shocks = jnp.concatenate(
            [
                picks[l] + (spread_out[:, l * size : (l + 1) * size] if l < WINDOW - 1 else 0.0)
                for l in range(1, WINDOW)
            ],
            axis=1,
        )
        scaled = shocks * jnp.concatenate([process] * (WINDOW - 1), axis=1)
        fixed = raw(
            as_left(scaled, 1),
            jnp.concatenate([as_right(shocks, 1), psi_s[ahead]], axis=0),
            NT,
        )
        readings = jnp.concatenate(
            [
                picks[i] * noise + jnp.where(last_row, -obs_s[pl.ds(step + i, 1), :], 0.0)
                for i in range(WINDOW)
            ],
            axis=1,
        )
        every = jnp.concatenate(picks, axis=1).astype(BF)
        high, low = halves(readings)
        lowest = (readings - high.astype(F32) - low.astype(F32)).astype(BF)
        own_noise = raw(
            jnp.concatenate([high, low, lowest], axis=1),
            jnp.concatenate([every, every, every], axis=1),
            NT,
        )
        diagonal = (iota((SLOTS, SLOTS), 0) == iota((SLOTS, SLOTS), 1)) & (
            iota((SLOTS, SLOTS), 0) >= taken
        )
        own_noise = own_noise + diagonal.astype(F32)

        cov, trans = cov_s[...], trans_s[...]
        cov_right, trans_right = as_right(cov, 0), as_right(trans, 0)
        seen = raw(as_left(watch, 1), jnp.concatenate([cov_right, trans_right], axis=1), NN)
        seen_cov = jnp.where(last_row, mean_s[...], seen[:, :size])
        seen_trans = jnp.where(last_row, pull_s[...], seen[:, size:])
        joint = fixed + raw(
            as_left(seen_cov, 1),
            jnp.concatenate([as_right(watch, 1), right_s[ahead]], axis=0),
            NT,
        )
        moved = raw(left_s[ahead], jnp.concatenate([cov_right, trans_right], axis=1), NN)
        moved_cov = raw(as_left(moved[:, :size], 1), right_s[ahead], NT) + added_s[ahead]
        square = joint[:, :SLOTS] + own_noise
        (to_state, to_trans), pivots, quad = eliminate(square, (joint[:, SLOTS:], seen_trans))
        mean_s[...] = to_state[SLOTS - 1 :, :]
        pull_s[...] = to_trans[SLOTS - 1 :, :]
        scale = jnp.where(last_row, 0.0, lax.rsqrt(pivots))
        factors = jnp.concatenate([to_state * scale, to_trans * scale], axis=1)
        outer = raw(as_left(factors, 0), as_right(factors, 0), TN)
        cov_s[...] = moved_cov - outer[:size, :size]
        trans_s[...] = moved[:, size:] - outer[:size, size:]
        info_s[...] = info_s[...] + outer[size:, size:]

        @pl.when(inside)
        def _():
            log_det = jnp.sum(jnp.log(pivots), axis=0, keepdims=True)
            count = taken.astype(F32) * LOG_TWO_PI
            kept_lik[mine] = kept_lik[mine] + (log_det + quad + count)

        return step + ahead, first + taken

    lax.while_loop(lambda state: state[0] < steps, body, (jnp.int32(0), jnp.int32(0)))

    info, pull = info_s[...], pull_s[...]
    for j in range(own - 1, -1, -1):
        cov = kept_cov[j]
        smooth_cov_ref[j] = cov - dot(dot(cov, info), cov)
        smooth_mean_ref[j : j + 1, :] = kept_mean[j] + dot(pull, cov)
        loglik_ref[j : j + 1, :] = kept_lik[j] * (-1.0 / (2.0 * size))
        if j > 0:
            trans = kept_trans[j]
            info = kept_info[j] + dot(dot(trans, info, TN), trans)
            pull = kept_pull[j] + dot(pull, trans)


def chain(position, gathered, prior_mean, prior_var, nw, damping, process_var, obs_var, own):
    steps, size = gathered.shape[0], gathered.shape[1] // 2
    padded = -(-(steps + WINDOW + 1) // 128) * 128
    wide = (WINDOW - 1) * size
    vmem = pl.BlockSpec(memory_space=pltpu.VMEM)
    square = (size, size)
    return pl.pallas_call(
        functools.partial(chain_kernel, own),
        out_shape=(
            jax.ShapeDtypeStruct((own, size), F32),
            jax.ShapeDtypeStruct((own, size, size), F32),
            jax.ShapeDtypeStruct((own, size), F32),
        ),
        in_specs=[pl.BlockSpec(memory_space=pltpu.SMEM)] + [vmem] * 7,
        out_specs=(vmem, vmem, vmem),
        scratch_shapes=[
            pltpu.VMEM((padded, size), F32),
            pltpu.VMEM((padded, size), F32),
            pltpu.VMEM((padded, size), jnp.int32),
            pltpu.VMEM((8, padded), jnp.int32),
            pltpu.SMEM((8, padded), jnp.int32),
            pltpu.VMEM((WINDOW + 1,) + square, F32),
            pltpu.VMEM((WINDOW + 1, size, 3 * size), BF),
            pltpu.VMEM((WINDOW + 1, size, 3 * size), BF),
            pltpu.VMEM((2 * wide, wide), BF),
            pltpu.VMEM((WINDOW + 1, size, 3 * wide), BF),
            pltpu.VMEM((WINDOW + 1,) + square, F32),
            pltpu.VMEM(square, F32),
            pltpu.VMEM(square, F32),
            pltpu.VMEM(square, F32),
            pltpu.VMEM((1, size), F32),
            pltpu.VMEM((1, size), F32),
            pltpu.VMEM((own,) + square, F32),
            pltpu.VMEM((own, 1, size), F32),
            pltpu.VMEM((own,) + square, F32),
            pltpu.VMEM((own,) + square, F32),
            pltpu.VMEM((own, 1, size), F32),
            pltpu.VMEM((own, 1, size), F32),
            pltpu.SemaphoreType.DMA(()),
        ],
        compiler_params=pltpu.CompilerParams(vmem_limit_bytes=48 * 1024 * 1024),
    )(position, gathered, prior_mean, prior_var, nw, damping, process_var, obs_var)


def gather_all(block, axis):
    size = lax.axis_size(axis)
    held, reach = block, 1
    if size & (size - 1):
        return lax.all_gather(block, axis, tiled=True), jnp.int32(0)
    while reach < size:
        pairs = [(i, i ^ reach) for i in range(size)]
        held = jnp.concatenate([held, lax.ppermute(held, axis, pairs)], axis=0)
        reach *= 2
    return held, lax.axis_index(axis).astype(jnp.int32)


def local(
    observed, obs_mask, prior_mean, prior_var, neighbor_weights, damping, process_var, obs_var
):
    own = observed.shape[0]
    block = jnp.concatenate([observed, obs_mask.astype(F32)], axis=1)
    gathered, flip = gather_all(block, "tm")
    position = jnp.stack([lax.axis_index("tm").astype(jnp.int32), flip])
    smooth_mean, smooth_cov, loglik = chain(
        position,
        gathered,
        prior_mean[None],
        prior_var[None],
        neighbor_weights,
        damping[None],
        process_var[None],
        obs_var[None],
        own,
    )
    return smooth_mean, smooth_cov, loglik[:, 0]


def solution(mesh):
    return jax.shard_map(
        local,
        mesh=mesh,
        in_specs=(
            P(("parts", "tm"), None),
            P(("parts", "tm"), None),
            P("parts"),
            P("parts"),
            P(),
            P(),
            P(),
            P(),
        ),
        out_specs=(P(("parts", "tm"), None), P(("parts", "tm"), None, None), P(("parts", "tm"))),
        check_vma=False,
    )
```

```python
import functools
import math

import jax
import jax.numpy as jnp
from jax import lax
from jax.experimental import pallas as pl
from jax.experimental.pallas import tpu as pltpu
from jax.sharding import PartitionSpec as P

GX = 16
GY = 8
OFFSETS = ((-1, -1), (-1, 0), (-1, 1), (0, -1), (0, 1), (1, -1), (1, 0), (1, 1))
LOG_TWO_PI = math.log(2.0 * math.pi)

WINDOW = 4
SLOTS = 32
FAR = 1 << 29

NN = (((1,), (0,)), ((), ()))
NT = (((1,), (1,)), ((), ()))
TN = (((0,), (0,)), ((), ()))
BF = jnp.bfloat16
F32 = jnp.float32


def halves(x):
    high = x.astype(BF)
    return high, (x - high.astype(F32)).astype(BF)


def as_left(x, axis):
    high, low = halves(x)
    return jnp.concatenate([high, high, low], axis=axis)


def as_right(x, axis):
    high, low = halves(x)
    return jnp.concatenate([high, low, high], axis=axis)


def raw(left, right, dims):
    return lax.dot_general(left, right, dims, preferred_element_type=F32)


def dot(left, right, dims=NN):
    (left_axis,), (right_axis,) = dims[0]
    return raw(as_left(left, left_axis), as_right(right, right_axis), dims)


def exact_dot(ones_left, right, dims=NN):
    (left_axis,), (right_axis,) = dims[0]
    high, low = halves(right)
    left = ones_left.astype(BF)
    return raw(
        jnp.concatenate([left, left], axis=left_axis),
        jnp.concatenate([high, low], axis=right_axis),
        dims,
    )


def iota(shape, axis):
    return lax.broadcasted_iota(jnp.int32, shape, axis)


def transition(nw, damping):
    size = GX * GY
    source, cell = iota((size, size), 0), iota((size, size), 1)
    row, column = cell // GY, cell % GY
    source_row, source_column = source // GY, source % GY
    centre = 1.0 - jnp.sum(nw, axis=0, keepdims=True) - damping
    flipped = jnp.where(source == cell, centre, 0.0)
    for index, (dx, dy) in enumerate(OFFSETS):
        hit = (source_row == row + dx) & (source_column == column + dy)
        flipped = flipped + jnp.where(hit, nw[index : index + 1, :], 0.0)
    return jnp.transpose(flipped)


def eliminate(square, sides):
    tiles = SLOTS // 8
    rows = iota((8, 128), 0)
    columns = {}
    for k in range(SLOTS - 1):
        for tile in range(k // 8, tiles):
            block = square[8 * tile : 8 * tile + 8, k : k + 1]
            columns[k, tile] = jnp.broadcast_to(block, (8, 128))
    parts = [[side[8 * t : 8 * t + 8, :] for t in range(tiles)] for side in sides]
    pivots = [jnp.ones((8, 128), F32) for _ in range(tiles)]
    quad = jnp.zeros((8, 128), F32)

    def spread(block, row):
        return jnp.broadcast_to(block[row : row + 1, :], (8, 128))

    for j in range(SLOTS - 1):
        home, row = divmod(j, 8)
        pivot = spread(columns[j, home], row)
        pivots[home] = jnp.where(rows == row, pivot, pivots[home])
        inverse = 1.0 / pivot
        weights = {}
        for tile in range(home, tiles):
            scaled = columns[j, tile] * inverse
            if tile == home:
                scaled = jnp.where(rows > row, scaled, 0.0)
            weights[tile] = scaled
        quad = quad + weights[tiles - 1] * columns[j, tiles - 1]
        for k in range(j + 1, SLOTS - 1):
            across = spread(columns[k, k // 8], row) if k // 8 == home else None
            if across is None:
                across = spread(columns[j, k // 8], k % 8)
            for tile in range(k // 8, tiles):
                columns[k, tile] = columns[k, tile] - weights[tile] * across
        for part in parts:
            across = spread(part[home], row)
            for tile in range(home, tiles):
                part[tile] = part[tile] - weights[tile] * across
    pivots = jnp.concatenate(pivots, axis=0)
    sides = [jnp.concatenate(part, axis=0) for part in parts]
    return sides, pivots, quad[7:8, :]


def chain_kernel(
    own,
    position_ref,
    gathered_ref,
    mean_ref,
    var_ref,
    nw_ref,
    damping_ref,
    process_ref,
    noise_ref,
    smooth_mean_ref,
    smooth_cov_ref,
    loglik_ref,
    mask_s,
    obs_s,
    rank_s,
    off_v,
    off_s,
    power_s,
    left_s,
    right_s,
    big_s,
    psi_s,
    added_s,
    cov_s,
    trans_s,
    info_s,
    mean_s,
    pull_s,
    kept_cov,
    kept_mean,
    kept_trans,
    kept_info,
    kept_pull,
    kept_lik,
    sem,
):
    size = GX * GY
    steps = gathered_ref.shape[0]
    padded = mask_s.shape[0]
    position = position_ref[0]
    base = position * own
    nw, damping = nw_ref[...], damping_ref[...]
    process, noise = process_ref[...], noise_ref[...]

    mask_s[...] = jnp.zeros_like(mask_s)
    obs_s[...] = jnp.zeros_like(obs_s)
    for block in range(steps // own):
        held = (position_ref[1] ^ block) * own
        for row in range(own):
            at = block * own + row
            line = gathered_ref[pl.ds(held + row, 1), :]
            obs_s[at : at + 1, :] = line[:, :size]
            mask_s[at : at + 1, :] = line[:, size:]
    mask = mask_s[...]
    mask_b = mask.astype(BF)
    before = (iota((padded, padded), 0) < iota((padded, padded), 1)).astype(BF)
    after = (iota((padded, padded), 0) > iota((padded, padded), 1)).astype(BF)
    counts_row = raw(jnp.ones((8, size), BF), mask_b, NT)
    off_v[...] = raw(counts_row.astype(BF), before, NN).astype(jnp.int32)
    copy = pltpu.make_async_copy(off_v, off_s, sem)
    copy.start()
    counts = raw(mask_b, jnp.ones((size, size), BF), NN)
    within = (iota((size, size), 0) < iota((size, size), 1)).astype(BF)
    rank = raw(mask_b, within, NN) + raw(after, counts.astype(BF), NN)
    rank_s[...] = jnp.where(mask > 0.0, rank.astype(jnp.int32), FAR)

    eye = (iota((size, size), 0) == iota((size, size), 1)).astype(F32)
    power_s[0] = eye
    power_s[1] = transition(nw, damping)
    for e in range(2, WINDOW + 1):
        power_s[e] = dot(power_s[(e + 1) // 2], power_s[e // 2])
    psi_s[...] = jnp.zeros_like(psi_s)
    big_s[...] = jnp.zeros_like(big_s)
    added_s[0] = jnp.zeros((size, size), F32)
    wide = (WINDOW - 1) * size
    for e in range(WINDOW + 1):
        left_s[e] = as_left(power_s[e], 1)
        right_s[e] = as_right(power_s[e], 1)
        if e >= 1:
            moved = power_s[e - 1]
            added_s[e] = added_s[e - 1] + dot(moved * process, moved, NT)
        for l in range(1, min(e, WINDOW - 1) + 1):
            high, low = halves(power_s[e - l])
            for piece, held in enumerate((high, low, high)):
                psi_s[e, :, piece * wide + (l - 1) * size : piece * wide + l * size] = held
    for i in range(1, WINDOW):
        for l in range(0, i):
            high, low = halves(power_s[i - l])
            for piece, held in enumerate((high, low)):
                start = piece * wide + (i - 1) * size
                big_s[start : start + size, l * size : (l + 1) * size] = held

    cov_s[...] = eye * var_ref[...]
    mean_s[...] = mean_ref[...]
    trans_s[...] = jnp.zeros_like(trans_s)
    info_s[...] = jnp.zeros_like(info_s)
    pull_s[...] = jnp.zeros_like(pull_s)
    kept_lik[...] = jnp.zeros_like(kept_lik)
    copy.wait()
    last_row = iota((SLOTS, 1), 0) == SLOTS - 1

    def body(state):
        step, first = state
        inside = (step >= base) & (step < base + own)
        cut = jnp.where(step < base, base, jnp.where(inside, step + 1, steps))
        end = jnp.minimum(step + WINDOW, cut)
        taken = jnp.minimum(off_s[0, end] - first, SLOTS - 1)
        ahead = jnp.int32(0)
        for i in range(1, WINDOW + 1):
            done = (step + i <= end) & (off_s[0, step + i] <= first + taken)
            ahead = ahead + done.astype(jnp.int32)
        mine = jnp.clip(step - base, 0, own - 1)

        @pl.when(inside & (first == off_s[0, step]))
        def _():
            kept_cov[mine] = cov_s[...]
            kept_mean[mine] = mean_s[...]
            kept_trans[mine] = trans_s[...]
            kept_info[mine] = info_s[...]
            kept_pull[mine] = pull_s[...]
            trans_s[...] = eye
            info_s[...] = jnp.zeros_like(info_s)
            pull_s[...] = jnp.zeros_like(pull_s)

        slot = iota((SLOTS, size), 0)
        picks = []
        for i in range(WINDOW):
            where = rank_s[pl.ds(step + i, 1), :] - first
            picks.append(jnp.where((slot == where) & (slot < taken), 1.0, 0.0))
        tail = jnp.concatenate(picks[1:], axis=1).astype(BF)
        spread_out = raw(jnp.concatenate([tail, tail], axis=1), big_s[...], NN)
        watch = picks[0] + spread_out[:, :size]
        shocks = jnp.concatenate(
            [
                picks[l] + (spread_out[:, l * size : (l + 1) * size] if l < WINDOW - 1 else 0.0)
                for l in range(1, WINDOW)
            ],
            axis=1,
        )
        scaled = shocks * jnp.concatenate([process] * (WINDOW - 1), axis=1)
        fixed = raw(
            as_left(scaled, 1),
            jnp.concatenate([as_right(shocks, 1), psi_s[ahead]], axis=0),
            NT,
        )
        readings = jnp.concatenate(
            [
                picks[i] * noise + jnp.where(last_row, -obs_s[pl.ds(step + i, 1), :], 0.0)
                for i in range(WINDOW)
            ],
            axis=1,
        )
        every = jnp.concatenate(picks, axis=1).astype(BF)
        high, low = halves(readings)
        lowest = (readings - high.astype(F32) - low.astype(F32)).astype(BF)
        own_noise = raw(
            jnp.concatenate([high, low, lowest], axis=1),
            jnp.concatenate([every, every, every], axis=1),
            NT,
        )
        diagonal = (iota((SLOTS, SLOTS), 0) == iota((SLOTS, SLOTS), 1)) & (
            iota((SLOTS, SLOTS), 0) >= taken
        )
        own_noise = own_noise + diagonal.astype(F32)

        cov, trans = cov_s[...], trans_s[...]
        cov_right, trans_right = as_right(cov, 0), as_right(trans, 0)
        seen = raw(as_left(watch, 1), jnp.concatenate([cov_right, trans_right], axis=1), NN)
        seen_cov = jnp.where(last_row, mean_s[...], seen[:, :size])
        seen_trans = jnp.where(last_row, pull_s[...], seen[:, size:])
        joint = fixed + raw(
            as_left(seen_cov, 1),
            jnp.concatenate([as_right(watch, 1), right_s[ahead]], axis=0),
            NT,
        )
        moved = raw(left_s[ahead], jnp.concatenate([cov_right, trans_right], axis=1), NN)
        moved_cov = raw(as_left(moved[:, :size], 1), right_s[ahead], NT) + added_s[ahead]
        square = joint[:, :SLOTS] + own_noise
        (to_state, to_trans), pivots, quad = eliminate(square, (joint[:, SLOTS:], seen_trans))
        mean_s[...] = to_state[SLOTS - 1 :, :]
        pull_s[...] = to_trans[SLOTS - 1 :, :]
        scale = jnp.where(last_row, 0.0, lax.rsqrt(pivots))
        factors = jnp.concatenate([to_state * scale, to_trans * scale], axis=1)
        outer = raw(as_left(factors, 0), as_right(factors, 0), TN)
        cov_s[...] = moved_cov - outer[:size, :size]
        trans_s[...] = moved[:, size:] - outer[:size, size:]
        info_s[...] = info_s[...] + outer[size:, size:]

        @pl.when(inside)
        def _():
            log_det = jnp.sum(jnp.log(pivots), axis=0, keepdims=True)
            count = taken.astype(F32) * LOG_TWO_PI
            kept_lik[mine] = kept_lik[mine] + (log_det + quad + count)

        return step + ahead, first + taken

    lax.while_loop(lambda state: state[0] < steps, body, (jnp.int32(0), jnp.int32(0)))

    info, pull = info_s[...], pull_s[...]
    for j in range(own - 1, -1, -1):
        cov = kept_cov[j]
        smooth_cov_ref[j] = cov - dot(dot(cov, info), cov)
        smooth_mean_ref[j : j + 1, :] = kept_mean[j] + dot(pull, cov)
        loglik_ref[j : j + 1, :] = kept_lik[j] * (-1.0 / (2.0 * size))
        if j > 0:
            trans = kept_trans[j]
            info = kept_info[j] + dot(dot(trans, info, TN), trans)
            pull = kept_pull[j] + dot(pull, trans)


def chain(position, gathered, prior_mean, prior_var, nw, damping, process_var, obs_var, own):
    steps, size = gathered.shape[0], gathered.shape[1] // 2
    padded = -(-(steps + WINDOW + 1) // 128) * 128
    wide = (WINDOW - 1) * size
    vmem = pl.BlockSpec(memory_space=pltpu.VMEM)
    square = (size, size)
    return pl.pallas_call(
        functools.partial(chain_kernel, own),
        out_shape=(
            jax.ShapeDtypeStruct((own, size), F32),
            jax.ShapeDtypeStruct((own, size, size), F32),
            jax.ShapeDtypeStruct((own, size), F32),
        ),
        in_specs=[pl.BlockSpec(memory_space=pltpu.SMEM)] + [vmem] * 7,
        out_specs=(vmem, vmem, vmem),
        scratch_shapes=[
            pltpu.VMEM((padded, size), F32),
            pltpu.VMEM((padded, size), F32),
            pltpu.VMEM((padded, size), jnp.int32),
            pltpu.VMEM((8, padded), jnp.int32),
            pltpu.SMEM((8, padded), jnp.int32),
            pltpu.VMEM((WINDOW + 1,) + square, F32),
            pltpu.VMEM((WINDOW + 1, size, 3 * size), BF),
            pltpu.VMEM((WINDOW + 1, size, 3 * size), BF),
            pltpu.VMEM((2 * wide, wide), BF),
            pltpu.VMEM((WINDOW + 1, size, 3 * wide), BF),
            pltpu.VMEM((WINDOW + 1,) + square, F32),
            pltpu.VMEM(square, F32),
            pltpu.VMEM(square, F32),
            pltpu.VMEM(square, F32),
            pltpu.VMEM((1, size), F32),
            pltpu.VMEM((1, size), F32),
            pltpu.VMEM((own,) + square, F32),
            pltpu.VMEM((own, 1, size), F32),
            pltpu.VMEM((own,) + square, F32),
            pltpu.VMEM((own,) + square, F32),
            pltpu.VMEM((own, 1, size), F32),
            pltpu.VMEM((own, 1, size), F32),
            pltpu.SemaphoreType.DMA(()),
        ],
        compiler_params=pltpu.CompilerParams(vmem_limit_bytes=48 * 1024 * 1024),
    )(position, gathered, prior_mean, prior_var, nw, damping, process_var, obs_var)


def gather_all(block, axis):
    size = lax.axis_size(axis)
    held, reach = block, 1
    if size & (size - 1):
        return lax.all_gather(block, axis, tiled=True), jnp.int32(0)
    while reach < size:
        pairs = [(i, i ^ reach) for i in range(size)]
        held = jnp.concatenate([held, lax.ppermute(held, axis, pairs)], axis=0)
        reach *= 2
    return held, lax.axis_index(axis).astype(jnp.int32)


def local(
    observed, obs_mask, prior_mean, prior_var, neighbor_weights, damping, process_var, obs_var
):
    own = observed.shape[0]
    block = jnp.concatenate([observed, obs_mask.astype(F32)], axis=1)
    gathered, flip = gather_all(block, "tm")
    position = jnp.stack([lax.axis_index("tm").astype(jnp.int32), flip])
    smooth_mean, smooth_cov, loglik = chain(
        position,
        gathered,
        prior_mean[None],
        prior_var[None],
        neighbor_weights,
        damping[None],
        process_var[None],
        obs_var[None],
        own,
    )
    return smooth_mean, smooth_cov, loglik[:, 0]


def solution(mesh):
    return jax.shard_map(
        local,
        mesh=mesh,
        in_specs=(
            P(("parts", "tm"), None),
            P(("parts", "tm"), None),
            P("parts"),
            P("parts"),
            P(),
            P(),
            P(),
            P(),
        ),
        out_specs=(P(("parts", "tm"), None), P(("parts", "tm"), None, None), P(("parts", "tm"))),
        check_vma=False,
    )
```

```python
import functools
import math

import jax
import jax.numpy as jnp
from jax import lax
from jax.experimental import pallas as pl
from jax.experimental.pallas import tpu as pltpu
from jax.sharding import PartitionSpec as P

GX = 16
GY = 8
OFFSETS = ((-1, -1), (-1, 0), (-1, 1), (0, -1), (0, 1), (1, -1), (1, 0), (1, 1))
LOG_TWO_PI = math.log(2.0 * math.pi)

WINDOW = 4
SLOTS = 32
FAR = 1 << 29

NN = (((1,), (0,)), ((), ()))
NT = (((1,), (1,)), ((), ()))
TN = (((0,), (0,)), ((), ()))
BF = jnp.bfloat16
F32 = jnp.float32


def halves(x):
    high = x.astype(BF)
    return high, (x - high.astype(F32)).astype(BF)


def as_left(x, axis):
    high, low = halves(x)
    return jnp.concatenate([high, high, low], axis=axis)


def as_right(x, axis):
    high, low = halves(x)
    return jnp.concatenate([high, low, high], axis=axis)


def raw(left, right, dims):
    return lax.dot_general(left, right, dims, preferred_element_type=F32)


def dot(left, right, dims=NN):
    (left_axis,), (right_axis,) = dims[0]
    return raw(as_left(left, left_axis), as_right(right, right_axis), dims)


def iota(shape, axis):
    return lax.broadcasted_iota(jnp.int32, shape, axis)


def transition(nw, damping):
    size = GX * GY
    source, cell = iota((size, size), 0), iota((size, size), 1)
    row, column = cell // GY, cell % GY
    source_row, source_column = source // GY, source % GY
    centre = 1.0 - jnp.sum(nw, axis=0, keepdims=True) - damping
    flipped = jnp.where(source == cell, centre, 0.0)
    for index, (dx, dy) in enumerate(OFFSETS):
        hit = (source_row == row + dx) & (source_column == column + dy)
        flipped = flipped + jnp.where(hit, nw[index : index + 1, :], 0.0)
    return jnp.transpose(flipped)


def eliminate(square, sides):
    tiles = SLOTS // 8
    rows = iota((8, 128), 0)
    columns = {}
    for k in range(SLOTS - 1):
        for tile in range(k // 8, tiles):
            block = square[8 * tile : 8 * tile + 8, k : k + 1]
            columns[k, tile] = jnp.broadcast_to(block, (8, 128))
    parts = [[side[8 * t : 8 * t + 8, :] for t in range(tiles)] for side in sides]
    pivots = [jnp.ones((8, 128), F32) for _ in range(tiles)]
    quad = jnp.zeros((8, 128), F32)

    def spread(block, row):
        return jnp.broadcast_to(block[row : row + 1, :], (8, 128))

    for j in range(SLOTS - 1):
        home, row = divmod(j, 8)
        pivot = spread(columns[j, home], row)
        pivots[home] = jnp.where(rows == row, pivot, pivots[home])
        inverse = 1.0 / pivot
        weights = {}
        for tile in range(home, tiles):
            scaled = columns[j, tile] * inverse
            if tile == home:
                scaled = jnp.where(rows > row, scaled, 0.0)
            weights[tile] = scaled
        quad = quad + weights[tiles - 1] * columns[j, tiles - 1]
        for k in range(j + 1, SLOTS - 1):
            across = spread(columns[k, k // 8], row) if k // 8 == home else None
            if across is None:
                across = spread(columns[j, k // 8], k % 8)
            for tile in range(k // 8, tiles):
                columns[k, tile] = columns[k, tile] - weights[tile] * across
        for part in parts:
            across = spread(part[home], row)
            for tile in range(home, tiles):
                part[tile] = part[tile] - weights[tile] * across
    pivots = jnp.concatenate(pivots, axis=0)
    sides = [jnp.concatenate(part, axis=0) for part in parts]
    return sides, pivots, quad[7:8, :]


def tables_kernel(
    nw_ref, damping_ref, process_ref, noise_ref, mean_ref, var_ref, strip_ref, big_ref, added_ref, line_ref
):
    size = GX * GY
    process = process_ref[...]
    line_ref[...] = jnp.concatenate(
        [mean_ref[...], var_ref[...], process, noise_ref[...], jnp.zeros((4, size), F32)], axis=0
    )
    powers = [
        (iota((size, size), 0) == iota((size, size), 1)).astype(F32),
        transition(nw_ref[...], damping_ref[...]),
    ]
    for e in range(2, WINDOW + 1):
        powers.append(dot(powers[(e + 1) // 2], powers[e // 2]))
    band = 3 * size
    strip_ref[...] = jnp.zeros_like(strip_ref)
    for e in range(WINDOW + 1):
        at = (WINDOW - e) * band
        strip_ref[:, at : at + band] = as_right(powers[e], 1)
    added_ref[0] = jnp.zeros((size, size), F32)
    added = jnp.zeros((size, size), F32)
    for e in range(1, WINDOW + 1):
        added = added + dot(powers[e - 1] * process, powers[e - 1], NT)
        added_ref[e] = added
    big_ref[...] = jnp.zeros_like(big_ref)
    wide = (WINDOW - 1) * size
    for i in range(1, WINDOW):
        for l in range(0, i):
            high, low = halves(powers[i - l])
            for piece, held in enumerate((high, low)):
                start = piece * wide + (i - 1) * size
                big_ref[start : start + size, l * size : (l + 1) * size] = held


def chain_kernel(
    own,
    position_ref,
    gathered_ref,
    strip_ref,
    big_ref,
    added_ref,
    line_ref,
    smooth_mean_ref,
    smooth_cov_ref,
    loglik_ref,
    mask_s,
    obs_s,
    rank_s,
    off_v,
    off_s,
    watch_s,
    fixed_s,
    noise_s,
    cov_s,
    trans_s,
    info_s,
    mean_s,
    pull_s,
    kept_cov,
    kept_mean,
    kept_trans,
    kept_info,
    kept_pull,
    kept_lik,
    sem,
):
    size = GX * GY
    steps = gathered_ref.shape[0]
    padded = mask_s.shape[0]
    position = position_ref[0]
    base = position * own
    process, noise = line_ref[2:3, :], line_ref[3:4, :]

    mask_s[...] = jnp.zeros_like(mask_s)
    obs_s[...] = jnp.zeros_like(obs_s)
    for block in range(steps // own):
        held = (position_ref[1] ^ block) * own
        for row in range(own):
            at = block * own + row
            line = gathered_ref[pl.ds(held + row, 1), :]
            obs_s[at : at + 1, :] = line[:, :size]
            mask_s[at : at + 1, :] = line[:, size:]
    mask = mask_s[...]
    mask_b = mask.astype(BF)
    before = (iota((padded, padded), 0) < iota((padded, padded), 1)).astype(BF)
    after = (iota((padded, padded), 0) > iota((padded, padded), 1)).astype(BF)
    counts_row = raw(jnp.ones((8, size), BF), mask_b, NT)
    off_v[...] = raw(counts_row.astype(BF), before, NN).astype(jnp.int32)
    copy = pltpu.make_async_copy(off_v, off_s, sem)
    copy.start()
    counts = raw(mask_b, jnp.ones((size, size), BF), NN)
    within = (iota((size, size), 0) < iota((size, size), 1)).astype(BF)
    rank = raw(mask_b, within, NN) + raw(after, counts.astype(BF), NN)
    rank_s[...] = jnp.where(mask > 0.0, rank.astype(jnp.int32), FAR)

    eye = (iota((size, size), 0) == iota((size, size), 1)).astype(F32)
    band = 3 * size
    cov_s[...] = eye * line_ref[1:2, :]
    mean_s[...] = line_ref[0:1, :]
    trans_s[...] = jnp.zeros_like(trans_s)
    info_s[...] = jnp.zeros_like(info_s)
    pull_s[...] = jnp.zeros_like(pull_s)
    kept_lik[...] = jnp.zeros_like(kept_lik)
    copy.wait()
    last_row = iota((SLOTS, 1), 0) == SLOTS - 1

    def is_own(step):
        return (step >= base) & (step < base + own)

    def extent(step, first):
        cut = jnp.where(step < base, base, jnp.where(is_own(step), step + 1, steps))
        end = jnp.minimum(step + WINDOW, cut)
        taken = jnp.minimum(off_s[0, end] - first, SLOTS - 1)
        ahead = jnp.int32(0)
        for i in range(1, WINDOW + 1):
            done = (step + i <= end) & (off_s[0, step + i] <= first + taken)
            ahead = ahead + done.astype(jnp.int32)
        return taken, ahead

    def power(e, count=1):
        return strip_ref[:, pl.ds(pl.multiple_of((WINDOW - e) * band, band), count * band)]

    def prepare(step, first, taken, ahead):
        slot = iota((SLOTS, size), 0)
        picks = []
        for i in range(WINDOW):
            where = rank_s[pl.ds(step + i, 1), :] - first
            picks.append(jnp.where((slot == where) & (slot < taken), 1.0, 0.0))
        tail = jnp.concatenate(picks[1:], axis=1).astype(BF)
        spread_out = raw(jnp.concatenate([tail, tail], axis=1), big_ref[...], NN)
        watch = as_right(picks[0] + spread_out[:, :size], 1)
        lefts, rights = [], []
        for l in range(1, WINDOW):
            shock = picks[l]
            if l < WINDOW - 1:
                shock = shock + spread_out[:, l * size : (l + 1) * size]
            lefts.append(as_left(shock * process, 1))
            rights.append(as_right(shock, 1))
        fixed = raw(
            jnp.concatenate(lefts, axis=1),
            jnp.concatenate(
                [jnp.concatenate(rights, axis=1), power(ahead - 1, WINDOW - 1)], axis=0
            ),
            NT,
        )
        readings = jnp.concatenate(
            [
                picks[i] * noise + jnp.where(last_row, -obs_s[pl.ds(step + i, 1), :], 0.0)
                for i in range(WINDOW)
            ],
            axis=1,
        )
        every = jnp.concatenate(picks, axis=1).astype(BF)
        high, low = halves(readings)
        lowest = (readings - high.astype(F32) - low.astype(F32)).astype(BF)
        own_noise = raw(
            jnp.concatenate([high, low, lowest], axis=1),
            jnp.concatenate([every, every, every], axis=1),
            NT,
        )
        diagonal = (iota((SLOTS, SLOTS), 0) == iota((SLOTS, SLOTS), 1)) & (
            iota((SLOTS, SLOTS), 0) >= taken
        )
        return watch, fixed[:, SLOTS:], fixed[:, :SLOTS] + own_noise + diagonal.astype(F32)

    zero = jnp.int32(0)
    opening = extent(zero, zero)
    watch_s[...], fixed_s[...], noise_s[...] = prepare(zero, zero, *opening)

    def body(state):
        step, first, taken, ahead = state
        inside = is_own(step)
        mine = jnp.clip(step - base, 0, own - 1)

        @pl.when(inside & (first == off_s[0, step]))
        def _():
            kept_cov[mine] = cov_s[...]
            kept_mean[mine] = mean_s[...]
            kept_trans[mine] = trans_s[...]
            kept_info[mine] = info_s[...]
            kept_pull[mine] = pull_s[...]
            trans_s[...] = eye
            info_s[...] = jnp.zeros_like(info_s)
            pull_s[...] = jnp.zeros_like(pull_s)

        both = as_left(jnp.concatenate([cov_s[...], trans_s[...]], axis=1), 0)
        watch = watch_s[...]
        seen = raw(watch, both, NN)
        seen_cov = jnp.where(last_row, mean_s[...], seen[:, :size])
        seen_trans = jnp.where(last_row, pull_s[...], seen[:, size:])
        moving = power(ahead)
        joint = raw(as_left(seen_cov, 1), jnp.concatenate([watch, moving], axis=0), NT)
        square = joint[:, :SLOTS] + noise_s[...]
        side = joint[:, SLOTS:] + fixed_s[...]
        moved = raw(moving, both, NN)
        moved_cov = raw(as_left(moved[:, :size], 1), moving, NT) + added_ref[ahead]

        next_step, next_first = step + ahead, first + taken
        following = extent(next_step, next_first)
        prepared = prepare(next_step, next_first, *following)

        (to_state, to_trans), pivots, quad = eliminate(square, (side, seen_trans))
        mean_s[...] = to_state[SLOTS - 1 :, :]
        pull_s[...] = to_trans[SLOTS - 1 :, :]
        scale = jnp.where(last_row, 0.0, lax.rsqrt(pivots))
        factors = jnp.concatenate([to_state * scale, to_trans * scale], axis=1)
        outer = raw(as_left(factors, 0), as_right(factors, 0), TN)
        cov_s[...] = moved_cov - outer[:size, :size]
        trans_s[...] = moved[:, size:] - outer[:size, size:]
        info_s[...] = info_s[...] + outer[size:, size:]
        watch_s[...], fixed_s[...], noise_s[...] = prepared

        @pl.when(inside)
        def _():
            log_det = jnp.sum(jnp.log(pivots), axis=0, keepdims=True)
            count = taken.astype(F32) * LOG_TWO_PI
            kept_lik[mine] = kept_lik[mine] + (log_det + quad + count)

        return (next_step, next_first) + following

    lax.while_loop(lambda state: state[0] < steps, body, (zero, zero) + opening)

    info, pull = info_s[...], pull_s[...]
    for j in range(own - 1, -1, -1):
        cov = kept_cov[j]
        smooth_cov_ref[j] = cov - dot(dot(cov, info), cov)
        smooth_mean_ref[j : j + 1, :] = kept_mean[j] + dot(pull, cov)
        loglik_ref[:, j : j + 1] = kept_lik[j][:, :1] * (-1.0 / (2.0 * size))
        if j > 0:
            trans = kept_trans[j]
            info = kept_info[j] + dot(dot(trans, info, TN), trans)
            pull = kept_pull[j] + dot(pull, trans)


VMEM = pl.BlockSpec(memory_space=pltpu.VMEM)
LIMIT = 48 * 1024 * 1024


def tables(nw, damping, process_var, obs_var, prior_mean, prior_var):
    size = nw.shape[1]
    wide = (WINDOW - 1) * size
    return pl.pallas_call(
        tables_kernel,
        out_shape=(
            jax.ShapeDtypeStruct((size, 2 * WINDOW * 3 * size), BF),
            jax.ShapeDtypeStruct((2 * wide, wide), BF),
            jax.ShapeDtypeStruct((WINDOW + 1, size, size), F32),
            jax.ShapeDtypeStruct((8, size), F32),
        ),
        in_specs=[VMEM] * 6,
        out_specs=(VMEM,) * 4,
        compiler_params=pltpu.CompilerParams(vmem_limit_bytes=LIMIT),
        cost_estimate=pl.CostEstimate(flops=10**8, bytes_accessed=2 * 10**6, transcendentals=0),
    )(nw, damping, process_var, obs_var, prior_mean, prior_var)


def chain(position, gathered, strip, big, added, line, own):
    steps, size = gathered.shape[0], gathered.shape[1] // 2
    padded = -(-(steps + WINDOW + 1) // 128) * 128
    square = (size, size)
    return pl.pallas_call(
        functools.partial(chain_kernel, own),
        out_shape=(
            jax.ShapeDtypeStruct((own, size), F32),
            jax.ShapeDtypeStruct((own, size, size), F32),
            jax.ShapeDtypeStruct((1, own), F32),
        ),
        in_specs=[pl.BlockSpec(memory_space=pltpu.SMEM)] + [VMEM] * 5,
        out_specs=(VMEM,) * 3,
        scratch_shapes=[
            pltpu.VMEM((padded, size), F32),
            pltpu.VMEM((padded, size), F32),
            pltpu.VMEM((padded, size), jnp.int32),
            pltpu.VMEM((8, padded), jnp.int32),
            pltpu.SMEM((8, padded), jnp.int32),
            pltpu.VMEM((SLOTS, 3 * size), BF),
            pltpu.VMEM((SLOTS, size), F32),
            pltpu.VMEM((SLOTS, SLOTS), F32),
            pltpu.VMEM(square, F32),
            pltpu.VMEM(square, F32),
            pltpu.VMEM(square, F32),
            pltpu.VMEM((1, size), F32),
            pltpu.VMEM((1, size), F32),
            pltpu.VMEM((own,) + square, F32),
            pltpu.VMEM((own, 1, size), F32),
            pltpu.VMEM((own,) + square, F32),
            pltpu.VMEM((own,) + square, F32),
            pltpu.VMEM((own, 1, size), F32),
            pltpu.VMEM((own, 1, size), F32),
            pltpu.SemaphoreType.DMA(()),
        ],
        compiler_params=pltpu.CompilerParams(vmem_limit_bytes=LIMIT),
    )(position, gathered, strip, big, added, line)


def gather_all(block, axis):
    size = lax.axis_size(axis)
    held, reach = block, 1
    if size & (size - 1):
        return lax.all_gather(block, axis, tiled=True), jnp.int32(0)
    while reach < size:
        pairs = [(i, i ^ reach) for i in range(size)]
        held = jnp.concatenate([held, lax.ppermute(held, axis, pairs)], axis=0)
        reach *= 2
    return held, lax.axis_index(axis).astype(jnp.int32)


def local(
    observed, obs_mask, prior_mean, prior_var, neighbor_weights, damping, process_var, obs_var
):
    own = observed.shape[0]
    block = jnp.concatenate([observed, obs_mask.astype(F32)], axis=1)
    gathered, flip = gather_all(block, "tm")
    position = jnp.stack([lax.axis_index("tm").astype(jnp.int32), flip])
    made = tables(
        neighbor_weights, damping[None], process_var[None], obs_var[None], prior_mean[None], prior_var[None]
    )
    smooth_mean, smooth_cov, loglik = chain(position, gathered, *made, own)
    return smooth_mean, smooth_cov, loglik.reshape(own)


def solution(mesh):
    return jax.shard_map(
        local,
        mesh=mesh,
        in_specs=(
            P(("parts", "tm"), None),
            P(("parts", "tm"), None),
            P("parts"),
            P("parts"),
            P(),
            P(),
            P(),
            P(),
        ),
        out_specs=(P(("parts", "tm"), None), P(("parts", "tm"), None, None), P(("parts", "tm"))),
        check_vma=False,
    )
```

```python
import functools
import math

import jax
import jax.numpy as jnp
from jax import lax
from jax.experimental import pallas as pl
from jax.experimental.pallas import tpu as pltpu
from jax.sharding import PartitionSpec as P

GX = 16
GY = 8
OFFSETS = ((-1, -1), (-1, 0), (-1, 1), (0, -1), (0, 1), (1, -1), (1, 0), (1, 1))
LOG_TWO_PI = math.log(2.0 * math.pi)

WINDOW = 4
SLOTS = 32
FAR = 1 << 29

NN = (((1,), (0,)), ((), ()))
NT = (((1,), (1,)), ((), ()))
TN = (((0,), (0,)), ((), ()))
BF = jnp.bfloat16
F32 = jnp.float32


def halves(x):
    high = x.astype(BF)
    return high, (x - high.astype(F32)).astype(BF)


def as_left(x, axis):
    high, low = halves(x)
    return jnp.concatenate([high, high, low], axis=axis)


def as_right(x, axis):
    high, low = halves(x)
    return jnp.concatenate([high, low, high], axis=axis)


def raw(left, right, dims):
    return lax.dot_general(left, right, dims, preferred_element_type=F32)


def dot(left, right, dims=NN):
    (left_axis,), (right_axis,) = dims[0]
    return raw(as_left(left, left_axis), as_right(right, right_axis), dims)


def iota(shape, axis):
    return lax.broadcasted_iota(jnp.int32, shape, axis)


def transition(nw, damping):
    size = GX * GY
    source, cell = iota((size, size), 0), iota((size, size), 1)
    row, column = cell // GY, cell % GY
    source_row, source_column = source // GY, source % GY
    centre = 1.0 - jnp.sum(nw, axis=0, keepdims=True) - damping
    flipped = jnp.where(source == cell, centre, 0.0)
    for index, (dx, dy) in enumerate(OFFSETS):
        hit = (source_row == row + dx) & (source_column == column + dy)
        flipped = flipped + jnp.where(hit, nw[index : index + 1, :], 0.0)
    return jnp.transpose(flipped)


def eliminate(square, sides):
    tiles = SLOTS // 8
    rows = iota((8, 128), 0)
    columns = {}
    for k in range(SLOTS - 1):
        for tile in range(k // 8, tiles):
            block = square[8 * tile : 8 * tile + 8, k : k + 1]
            columns[k, tile] = jnp.broadcast_to(block, (8, 128))
    parts = [[side[8 * t : 8 * t + 8, :] for t in range(tiles)] for side in sides]
    pivots = [jnp.ones((8, 128), F32) for _ in range(tiles)]
    quad = jnp.zeros((8, 128), F32)

    def spread(block, row):
        return jnp.broadcast_to(block[row : row + 1, :], (8, 128))

    for j in range(SLOTS - 1):
        home, row = divmod(j, 8)
        pivot = spread(columns[j, home], row)
        pivots[home] = jnp.where(rows == row, pivot, pivots[home])
        inverse = 1.0 / pivot
        weights = {}
        for tile in range(home, tiles):
            scaled = columns[j, tile] * inverse
            if tile == home:
                scaled = jnp.where(rows > row, scaled, 0.0)
            weights[tile] = scaled
        quad = quad + weights[tiles - 1] * columns[j, tiles - 1]
        for k in range(j + 1, SLOTS - 1):
            across = spread(columns[k, k // 8], row) if k // 8 == home else None
            if across is None:
                across = spread(columns[j, k // 8], k % 8)
            for tile in range(k // 8, tiles):
                columns[k, tile] = columns[k, tile] - weights[tile] * across
        for part in parts:
            across = spread(part[home], row)
            for tile in range(home, tiles):
                part[tile] = part[tile] - weights[tile] * across
    pivots = jnp.concatenate(pivots, axis=0)
    sides = [jnp.concatenate(part, axis=0) for part in parts]
    return sides, pivots, quad[7:8, :]


def tables_kernel(
    nw_ref, damping_ref, process_ref, noise_ref, mean_ref, var_ref, strip_ref, big_ref, added_ref, line_ref
):
    size = GX * GY
    process = process_ref[...]
    line_ref[...] = jnp.concatenate(
        [mean_ref[...], var_ref[...], process, noise_ref[...], jnp.zeros((4, size), F32)], axis=0
    )
    powers = [
        (iota((size, size), 0) == iota((size, size), 1)).astype(F32),
        transition(nw_ref[...], damping_ref[...]),
    ]
    for e in range(2, WINDOW + 1):
        powers.append(dot(powers[(e + 1) // 2], powers[e // 2]))
    band = 3 * size
    strip_ref[...] = jnp.zeros_like(strip_ref)
    for e in range(WINDOW + 1):
        at = (WINDOW - e) * band
        strip_ref[:, at : at + band] = as_right(powers[e], 1)
    added_ref[0] = jnp.zeros((size, size), F32)
    added = jnp.zeros((size, size), F32)
    for e in range(1, WINDOW + 1):
        added = added + dot(powers[e - 1] * process, powers[e - 1], NT)
        added_ref[e] = added
    for i in range(1, WINDOW):
        high, low = halves(powers[i])
        big_ref[:size, (i - 1) * size : i * size] = high
        big_ref[size:, (i - 1) * size : i * size] = low


def chain_kernel(
    own,
    position_ref,
    gathered_ref,
    strip_ref,
    big_ref,
    added_ref,
    line_ref,
    smooth_mean_ref,
    smooth_cov_ref,
    loglik_ref,
    mask_s,
    obs_s,
    rank_s,
    off_v,
    off_s,
    watch_s,
    fixed_s,
    noise_s,
    cov_s,
    trans_s,
    info_s,
    mean_s,
    pull_s,
    kept_cov,
    kept_mean,
    kept_trans,
    kept_info,
    kept_pull,
    kept_lik,
    sem,
):
    size = GX * GY
    steps = gathered_ref.shape[0]
    padded = mask_s.shape[0]
    position = position_ref[0]
    base = position * own
    process, noise = line_ref[2:3, :], line_ref[3:4, :]

    mask_s[...] = jnp.zeros_like(mask_s)
    obs_s[...] = jnp.zeros_like(obs_s)
    for block in range(steps // own):
        held = (position_ref[1] ^ block) * own
        for row in range(own):
            at = block * own + row
            line = gathered_ref[pl.ds(held + row, 1), :]
            obs_s[at : at + 1, :] = line[:, :size]
            mask_s[at : at + 1, :] = line[:, size:]
    mask = mask_s[...]
    mask_b = mask.astype(BF)
    before = (iota((padded, padded), 0) < iota((padded, padded), 1)).astype(BF)
    after = (iota((padded, padded), 0) > iota((padded, padded), 1)).astype(BF)
    counts_row = raw(jnp.ones((8, size), BF), mask_b, NT)
    off_v[...] = raw(counts_row.astype(BF), before, NN).astype(jnp.int32)
    copy = pltpu.make_async_copy(off_v, off_s, sem)
    copy.start()
    counts = raw(mask_b, jnp.ones((size, size), BF), NN)
    within = (iota((size, size), 0) < iota((size, size), 1)).astype(BF)
    rank = raw(mask_b, within, NN) + raw(after, counts.astype(BF), NN)
    rank_s[...] = jnp.where(mask > 0.0, rank.astype(jnp.int32), FAR)

    eye = (iota((size, size), 0) == iota((size, size), 1)).astype(F32)
    band = 3 * size
    cov_s[...] = eye * line_ref[1:2, :]
    mean_s[...] = line_ref[0:1, :]
    trans_s[...] = jnp.zeros_like(trans_s)
    info_s[...] = jnp.zeros_like(info_s)
    pull_s[...] = jnp.zeros_like(pull_s)
    kept_lik[...] = jnp.zeros_like(kept_lik)
    copy.wait()
    last_row = iota((SLOTS, 1), 0) == SLOTS - 1

    def is_own(step):
        return (step >= base) & (step < base + own)

    def extent(step, first):
        cut = jnp.where(step < base, base, jnp.where(is_own(step), step + 1, steps))
        end = jnp.minimum(step + WINDOW, cut)
        taken = jnp.minimum(off_s[0, end] - first, SLOTS - 1)
        ahead = jnp.int32(0)
        for i in range(1, WINDOW + 1):
            done = (step + i <= end) & (off_s[0, step + i] <= first + taken)
            ahead = ahead + done.astype(jnp.int32)
        return taken, ahead

    def power(e, count=1):
        return strip_ref[:, pl.ds(pl.multiple_of((WINDOW - e) * band, band), count * band)]

    def prepare(step, first, taken, ahead):
        slot = iota((SLOTS, size), 0)
        picks = []
        for i in range(WINDOW):
            where = rank_s[pl.ds(step + i, 1), :] - first
            picks.append(jnp.where((slot == where) & (slot < taken), 1.0, 0.0))
        tail = jnp.concatenate(picks[1:], axis=0).astype(BF)
        rows = raw(jnp.concatenate([tail, tail], axis=1), big_ref[...], NN)

        def moved_pick(i, e):
            if e == 0:
                return picks[i]
            return rows[(i - 1) * SLOTS : i * SLOTS, (e - 1) * size : e * size]

        watch = as_right(sum(moved_pick(i, i) for i in range(WINDOW)), 1)
        lefts, rights = [], []
        for l in range(1, WINDOW):
            shock = sum(moved_pick(i, i - l) for i in range(l, WINDOW))
            lefts.append(as_left(shock * process, 1))
            rights.append(as_right(shock, 1))
        fixed = raw(
            jnp.concatenate(lefts, axis=1),
            jnp.concatenate(
                [jnp.concatenate(rights, axis=1), power(ahead - 1, WINDOW - 1)], axis=0
            ),
            NT,
        )
        readings = sum(picks[i] * obs_s[pl.ds(step + i, 1), :] for i in range(WINDOW))
        readings = jnp.sum(readings, axis=1, keepdims=True)
        variances = jnp.sum(sum(picks) * noise, axis=1, keepdims=True)
        variances = variances + (iota((SLOTS, 1), 0) >= taken).astype(F32)
        diagonal = iota((SLOTS, SLOTS), 0) == iota((SLOTS, SLOTS), 1)
        across = jnp.sum(jnp.where(diagonal, readings, 0.0), axis=0, keepdims=True)
        own_noise = jnp.where(diagonal, variances, 0.0) - jnp.where(last_row, across, 0.0)
        return watch, fixed[:, SLOTS:], fixed[:, :SLOTS] + own_noise

    zero = jnp.int32(0)
    opening = extent(zero, zero)
    watch_s[...], fixed_s[...], noise_s[...] = prepare(zero, zero, *opening)

    def body(state):
        step, first, taken, ahead = state
        inside = is_own(step)
        mine = jnp.clip(step - base, 0, own - 1)

        @pl.when(inside & (first == off_s[0, step]))
        def _():
            kept_cov[mine] = cov_s[...]
            kept_mean[mine] = mean_s[...]
            kept_trans[mine] = trans_s[...]
            kept_info[mine] = info_s[...]
            kept_pull[mine] = pull_s[...]
            trans_s[...] = eye
            info_s[...] = jnp.zeros_like(info_s)
            pull_s[...] = jnp.zeros_like(pull_s)

        both = as_left(jnp.concatenate([cov_s[...], trans_s[...]], axis=1), 0)
        watch, moving = watch_s[...], power(ahead)
        both_cov, both_trans = both[:, :size], both[:, size:]
        seen_cov = jnp.where(last_row, mean_s[...], raw(watch, both_cov, NN))
        seen_trans = jnp.where(last_row, pull_s[...], raw(watch, both_trans, NN))
        seen_left = as_left(seen_cov, 1)
        square = raw(seen_left, watch, NT) + noise_s[...]
        side = raw(seen_left, moving, NT) + fixed_s[...]
        moved = raw(moving, both, NN)
        moved_cov = raw(as_left(moved[:, :size], 1), moving, NT) + added_ref[ahead]

        next_step, next_first = step + ahead, first + taken
        following = extent(next_step, next_first)
        prepared = prepare(next_step, next_first, *following)

        (to_state, to_trans), pivots, quad = eliminate(square, (side, seen_trans))
        mean_s[...] = to_state[SLOTS - 1 :, :]
        pull_s[...] = to_trans[SLOTS - 1 :, :]
        scale = jnp.where(last_row, 0.0, lax.rsqrt(pivots))
        gain, reach = to_state * scale, to_trans * scale
        gain_left, reach_right = as_left(gain, 0), as_right(reach, 0)
        cov_s[...] = moved_cov - raw(gain_left, as_right(gain, 0), TN)
        trans_s[...] = moved[:, size:] - raw(gain_left, reach_right, TN)
        info_s[...] = info_s[...] + raw(as_left(reach, 0), reach_right, TN)
        watch_s[...], fixed_s[...], noise_s[...] = prepared

        @pl.when(inside)
        def _():
            log_det = jnp.sum(jnp.log(pivots), axis=0, keepdims=True)
            count = taken.astype(F32) * LOG_TWO_PI
            kept_lik[mine] = kept_lik[mine] + (log_det + quad + count)

        return (next_step, next_first) + following

    lax.while_loop(lambda state: state[0] < steps, body, (zero, zero) + opening)

    info, pull = info_s[...], pull_s[...]
    for j in range(own - 1, -1, -1):
        cov = kept_cov[j]
        smooth_cov_ref[j] = cov - dot(dot(cov, info), cov)
        smooth_mean_ref[j : j + 1, :] = kept_mean[j] + dot(pull, cov)
        loglik_ref[:, j : j + 1] = kept_lik[j][:, :1] * (-1.0 / (2.0 * size))
        if j > 0:
            trans = kept_trans[j]
            info = kept_info[j] + dot(dot(trans, info, TN), trans)
            pull = kept_pull[j] + dot(pull, trans)


VMEM = pl.BlockSpec(memory_space=pltpu.VMEM)
LIMIT = 48 * 1024 * 1024


def tables(nw, damping, process_var, obs_var, prior_mean, prior_var):
    size = nw.shape[1]
    return pl.pallas_call(
        tables_kernel,
        out_shape=(
            jax.ShapeDtypeStruct((size, 2 * WINDOW * 3 * size), BF),
            jax.ShapeDtypeStruct((2 * size, (WINDOW - 1) * size), BF),
            jax.ShapeDtypeStruct((WINDOW + 1, size, size), F32),
            jax.ShapeDtypeStruct((8, size), F32),
        ),
        in_specs=[VMEM] * 6,
        out_specs=(VMEM,) * 4,
        compiler_params=pltpu.CompilerParams(vmem_limit_bytes=LIMIT),
        cost_estimate=pl.CostEstimate(flops=10**8, bytes_accessed=2 * 10**6, transcendentals=0),
    )(nw, damping, process_var, obs_var, prior_mean, prior_var)


def chain(position, gathered, strip, big, added, line, own):
    steps, size = gathered.shape[0], gathered.shape[1] // 2
    padded = -(-(steps + WINDOW + 1) // 128) * 128
    square = (size, size)
    return pl.pallas_call(
        functools.partial(chain_kernel, own),
        out_shape=(
            jax.ShapeDtypeStruct((own, size), F32),
            jax.ShapeDtypeStruct((own, size, size), F32),
            jax.ShapeDtypeStruct((1, own), F32),
        ),
        in_specs=[pl.BlockSpec(memory_space=pltpu.SMEM)] + [VMEM] * 5,
        out_specs=(VMEM,) * 3,
        scratch_shapes=[
            pltpu.VMEM((padded, size), F32),
            pltpu.VMEM((padded, size), F32),
            pltpu.VMEM((padded, size), jnp.int32),
            pltpu.VMEM((8, padded), jnp.int32),
            pltpu.SMEM((8, padded), jnp.int32),
            pltpu.VMEM((SLOTS, 3 * size), BF),
            pltpu.VMEM((SLOTS, size), F32),
            pltpu.VMEM((SLOTS, SLOTS), F32),
            pltpu.VMEM(square, F32),
            pltpu.VMEM(square, F32),
            pltpu.VMEM(square, F32),
            pltpu.VMEM((1, size), F32),
            pltpu.VMEM((1, size), F32),
            pltpu.VMEM((own,) + square, F32),
            pltpu.VMEM((own, 1, size), F32),
            pltpu.VMEM((own,) + square, F32),
            pltpu.VMEM((own,) + square, F32),
            pltpu.VMEM((own, 1, size), F32),
            pltpu.VMEM((own, 1, size), F32),
            pltpu.SemaphoreType.DMA(()),
        ],
        compiler_params=pltpu.CompilerParams(vmem_limit_bytes=LIMIT),
    )(position, gathered, strip, big, added, line)


def gather_all(block, axis):
    size = lax.axis_size(axis)
    held, reach = block, 1
    if size & (size - 1):
        return lax.all_gather(block, axis, tiled=True), jnp.int32(0)
    while reach < size:
        pairs = [(i, i ^ reach) for i in range(size)]
        held = jnp.concatenate([held, lax.ppermute(held, axis, pairs)], axis=0)
        reach *= 2
    return held, lax.axis_index(axis).astype(jnp.int32)


def local(
    observed, obs_mask, prior_mean, prior_var, neighbor_weights, damping, process_var, obs_var
):
    own = observed.shape[0]
    block = jnp.concatenate([observed, obs_mask.astype(F32)], axis=1)
    gathered, flip = gather_all(block, "tm")
    position = jnp.stack([lax.axis_index("tm").astype(jnp.int32), flip])
    made = tables(
        neighbor_weights, damping[None], process_var[None], obs_var[None], prior_mean[None], prior_var[None]
    )
    smooth_mean, smooth_cov, loglik = chain(position, gathered, *made, own)
    return smooth_mean, smooth_cov, loglik.reshape(own)


def solution(mesh):
    return jax.shard_map(
        local,
        mesh=mesh,
        in_specs=(
            P(("parts", "tm"), None),
            P(("parts", "tm"), None),
            P("parts"),
            P("parts"),
            P(),
            P(),
            P(),
            P(),
        ),
        out_specs=(P(("parts", "tm"), None), P(("parts", "tm"), None, None), P(("parts", "tm"))),
        check_vma=False,
    )
```

```python
import functools
import math

import jax
import jax.numpy as jnp
from jax import lax
from jax.experimental import pallas as pl
from jax.experimental.pallas import tpu as pltpu
from jax.sharding import PartitionSpec as P

GX = 16
GY = 8
OFFSETS = ((-1, -1), (-1, 0), (-1, 1), (0, -1), (0, 1), (1, -1), (1, 0), (1, 1))
LOG_TWO_PI = math.log(2.0 * math.pi)

WINDOW = 5
SLOTS = 32
FAR = 1 << 29

NN = (((1,), (0,)), ((), ()))
NT = (((1,), (1,)), ((), ()))
TN = (((0,), (0,)), ((), ()))
BF = jnp.bfloat16
F32 = jnp.float32


def halves(x):
    high = x.astype(BF)
    return high, (x - high.astype(F32)).astype(BF)


def as_left(x, axis):
    high, low = halves(x)
    return jnp.concatenate([high, high, low], axis=axis)


def as_right(x, axis):
    high, low = halves(x)
    return jnp.concatenate([high, low, high], axis=axis)


def raw(left, right, dims):
    return lax.dot_general(left, right, dims, preferred_element_type=F32)


def dot(left, right, dims=NN):
    (left_axis,), (right_axis,) = dims[0]
    return raw(as_left(left, left_axis), as_right(right, right_axis), dims)


def iota(shape, axis):
    return lax.broadcasted_iota(jnp.int32, shape, axis)


def transition(nw, damping):
    size = GX * GY
    source, cell = iota((size, size), 0), iota((size, size), 1)
    row, column = cell // GY, cell % GY
    source_row, source_column = source // GY, source % GY
    centre = 1.0 - jnp.sum(nw, axis=0, keepdims=True) - damping
    flipped = jnp.where(source == cell, centre, 0.0)
    for index, (dx, dy) in enumerate(OFFSETS):
        hit = (source_row == row + dx) & (source_column == column + dy)
        flipped = flipped + jnp.where(hit, nw[index : index + 1, :], 0.0)
    return jnp.transpose(flipped)


def eliminate(square, sides):
    tiles = SLOTS // 8
    rows, lanes = iota((8, 128), 0), iota((8, 128), 1)
    columns = {}
    for k in range(SLOTS - 1):
        for tile in range(k // 8, tiles):
            block = square[8 * tile : 8 * tile + 8, k : k + 1]
            columns[k, tile] = jnp.broadcast_to(block, (8, 128))
    parts = [[side[8 * t : 8 * t + 8, :] for t in range(tiles)] for side in sides]
    pivots = [jnp.ones((8, 128), F32) for _ in range(tiles)]
    quad = jnp.zeros((8, 128), F32)

    def spread(block, row):
        return jnp.broadcast_to(block[row : row + 1, :], (8, 128))

    for j in range(SLOTS - 1):
        home, row = divmod(j, 8)
        pivot = spread(columns[j, home], row)
        pivots[home] = jnp.where(rows == row, pivot, pivots[home])
        inverse = 1.0 / pivot
        weights = {}
        for tile in range(home, tiles):
            scaled = columns[j, tile] * inverse
            if tile == home:
                scaled = jnp.where(rows > row, scaled, 0.0)
            weights[tile] = scaled
        quad = jnp.where(lanes == j, weights[tiles - 1] * columns[j, tiles - 1], quad)
        for k in range(j + 1, SLOTS - 1):
            across = spread(columns[k, k // 8], row) if k // 8 == home else None
            if across is None:
                across = spread(columns[j, k // 8], k % 8)
            for tile in range(k // 8, tiles):
                columns[k, tile] = columns[k, tile] - weights[tile] * across
        for part in parts:
            across = jnp.broadcast_to(part[home][row : row + 1, :], part[home].shape)
            for tile in range(home, tiles):
                part[tile] = part[tile] - weights[tile][:, : part[tile].shape[1]] * across
    pivots = jnp.concatenate(pivots, axis=0)
    sides = [jnp.concatenate(part, axis=0) for part in parts]
    return sides, pivots, quad[7:8, :]


def tables_kernel(
    nw_ref, damping_ref, process_ref, noise_ref, mean_ref, var_ref, strip_ref, big_ref, added_ref, line_ref
):
    size = GX * GY
    process = process_ref[...]
    line_ref[...] = jnp.concatenate(
        [mean_ref[...], var_ref[...], process, noise_ref[...], jnp.zeros((4, size), F32)], axis=0
    )
    powers = [
        (iota((size, size), 0) == iota((size, size), 1)).astype(F32),
        transition(nw_ref[...], damping_ref[...]),
    ]
    for e in range(2, WINDOW + 1):
        powers.append(dot(powers[(e + 1) // 2], powers[e // 2]))
    band = 3 * size
    strip_ref[...] = jnp.zeros_like(strip_ref)
    for e in range(WINDOW + 1):
        at = (WINDOW - e) * band
        strip_ref[:, at : at + band] = as_right(powers[e], 1)
    added_ref[0] = jnp.zeros((size, size), F32)
    added = jnp.zeros((size, size), F32)
    for e in range(1, WINDOW + 1):
        added = added + dot(powers[e - 1] * process, powers[e - 1], NT)
        added_ref[e] = added
    for i in range(1, WINDOW):
        high, low = halves(powers[i])
        big_ref[:size, (i - 1) * size : i * size] = high
        big_ref[size:, (i - 1) * size : i * size] = low


def chain_kernel(
    own,
    position_ref,
    gathered_ref,
    strip_ref,
    big_ref,
    added_ref,
    line_ref,
    smooth_mean_ref,
    smooth_cov_ref,
    loglik_ref,
    mask_s,
    obs_s,
    rank_s,
    off_v,
    off_s,
    watch_s,
    fixed_s,
    square_s,
    carry_s,
    cross_s,
    noise_s,
    next_watch_s,
    next_fixed_s,
    cov_s,
    trans_s,
    info_s,
    mean_s,
    pull_s,
    kept_cov,
    kept_mean,
    kept_trans,
    kept_info,
    kept_pull,
    kept_lik,
    sem,
):
    size = GX * GY
    steps = gathered_ref.shape[0]
    padded = mask_s.shape[0]
    position = position_ref[0]
    base = position * own
    process, noise = line_ref[2:3, :], line_ref[3:4, :]

    mask_s[...] = jnp.zeros_like(mask_s)
    obs_s[...] = jnp.zeros_like(obs_s)
    for block in range(steps // own):
        held = (position_ref[1] ^ block) * own
        for row in range(own):
            at = block * own + row
            line = gathered_ref[pl.ds(held + row, 1), :]
            obs_s[at : at + 1, :] = line[:, :size]
            mask_s[at : at + 1, :] = line[:, size:]
    mask = mask_s[...]
    mask_b = mask.astype(BF)
    before = (iota((padded, padded), 0) < iota((padded, padded), 1)).astype(BF)
    after = (iota((padded, padded), 0) > iota((padded, padded), 1)).astype(BF)
    counts_row = raw(jnp.ones((8, size), BF), mask_b, NT)
    off_v[...] = raw(counts_row.astype(BF), before, NN).astype(jnp.int32)
    copy = pltpu.make_async_copy(off_v, off_s, sem)
    copy.start()
    counts = raw(mask_b, jnp.ones((size, size), BF), NN)
    within = (iota((size, size), 0) < iota((size, size), 1)).astype(BF)
    rank = raw(mask_b, within, NN) + raw(after, counts.astype(BF), NN)
    rank_s[...] = jnp.where(mask > 0.0, rank.astype(jnp.int32), FAR)

    eye = (iota((size, size), 0) == iota((size, size), 1)).astype(F32)
    band = 3 * size
    cov_s[...] = eye * line_ref[1:2, :]
    mean_s[...] = line_ref[0:1, :]
    trans_s[...] = jnp.zeros_like(trans_s)
    info_s[...] = jnp.zeros_like(info_s)
    pull_s[...] = jnp.zeros_like(pull_s)
    kept_lik[...] = jnp.zeros_like(kept_lik)
    copy.wait()
    last_row = iota((SLOTS, 1), 0) == SLOTS - 1

    def is_own(step):
        return (step >= base) & (step < base + own)

    def extent(step, first):
        last = base + own - 1
        cut = jnp.where(step < base, base, jnp.where(step < last, step + 1, steps))
        end = jnp.minimum(step + WINDOW, cut)
        taken = jnp.minimum(off_s[0, end] - first, SLOTS - 1)
        ahead = jnp.int32(0)
        for i in range(1, WINDOW + 1):
            done = (step + i <= end) & (off_s[0, step + i] <= first + taken)
            ahead = ahead + done.astype(jnp.int32)
        return taken, ahead

    def power(e, count=1):
        return strip_ref[:, pl.ds(pl.multiple_of((WINDOW - e) * band, band), count * band)]

    def prepare(step, first, taken, ahead):
        slot = iota((SLOTS, size), 0)
        picks = []
        for i in range(WINDOW):
            where = rank_s[pl.ds(step + i, 1), :] - first
            picks.append(jnp.where((slot == where) & (slot < taken), 1.0, 0.0))
        tail = jnp.concatenate(picks[1:], axis=0).astype(BF)
        rows = raw(jnp.concatenate([tail, tail], axis=1), big_ref[...], NN)

        def moved_pick(i, e):
            if e == 0:
                return picks[i]
            return rows[(i - 1) * SLOTS : i * SLOTS, (e - 1) * size : e * size]

        watch = as_right(sum(moved_pick(i, i) for i in range(WINDOW)), 1)
        lefts, rights = [], []
        for l in range(1, WINDOW):
            shock = sum(moved_pick(i, i - l) for i in range(l, WINDOW))
            lefts.append(as_left(shock * process, 1))
            rights.append(as_right(shock, 1))
        lefts = jnp.concatenate(lefts, axis=1)
        noise_part = raw(lefts, jnp.concatenate(rights, axis=1), NT)
        side_part = raw(lefts, power(ahead - 1, WINDOW - 1), NT)
        readings = sum(picks[i] * obs_s[pl.ds(step + i, 1), :] for i in range(WINDOW))
        readings = jnp.sum(readings, axis=1, keepdims=True)
        variances = jnp.sum(sum(picks) * noise, axis=1, keepdims=True)
        variances = variances + (iota((SLOTS, 1), 0) >= taken).astype(F32)
        diagonal = iota((SLOTS, SLOTS), 0) == iota((SLOTS, SLOTS), 1)
        across = jnp.sum(jnp.where(diagonal, readings, 0.0), axis=0, keepdims=True)
        own_noise = jnp.where(diagonal, variances, 0.0) - jnp.where(last_row, across, 0.0)
        return watch, side_part, noise_part + own_noise

    def link(ahead, fixed, watch, noise):
        at = pl.multiple_of((WINDOW - ahead) * band, band)
        high, low = strip_ref[:, pl.ds(at, size)], strip_ref[:, pl.ds(at + size, size)]
        rights = [jnp.concatenate([high, high, low], axis=0), as_left(added_ref[ahead], 0)]
        onward = raw(watch, jnp.concatenate(rights, axis=1), NN)
        both = raw(as_left(jnp.concatenate([fixed, onward[:, size:]], axis=0), 1), watch, NT)
        return as_right(onward[:, :size], 1), both[:SLOTS], noise + both[SLOTS:]

    zero = jnp.int32(0)
    opening = (zero, zero) + extent(zero, zero)
    second = (opening[3], opening[2])
    second = second + extent(*second)
    watch, fixed, noise_now = prepare(*opening)
    seen = jnp.where(last_row, mean_s[...], raw(watch, as_left(cov_s[...], 0), NN))
    square_s[...] = raw(as_left(seen, 1), watch, NT) + noise_now
    watch_s[...], fixed_s[...] = watch, fixed
    watch, next_fixed, noise_now = prepare(*second)
    next_watch_s[...], next_fixed_s[...] = watch, next_fixed
    carry_s[...], cross_s[...], noise_s[...] = link(opening[3], fixed, watch, noise_now)

    def body(state):
        step, first, taken, ahead = state[:4]
        inside = is_own(step)
        mine = jnp.clip(step - base, 0, own - 1)

        @pl.when(inside & (first == off_s[0, step]))
        def _():
            kept_cov[mine] = cov_s[...]
            kept_mean[mine] = mean_s[...]
            kept_trans[mine] = trans_s[...]
            kept_info[mine] = info_s[...]
            kept_pull[mine] = pull_s[...]
            trans_s[...] = eye
            info_s[...] = jnp.zeros_like(info_s)
            pull_s[...] = jnp.zeros_like(pull_s)

        square = square_s[...]
        two = 2 * SLOTS
        rows = jnp.concatenate([watch_s[...], carry_s[...], power(ahead)], axis=0)
        seen = raw(rows, as_left(jnp.concatenate([cov_s[...], trans_s[...]], axis=1), 0), NN)
        seen_cov = jnp.where(last_row, mean_s[...], seen[:SLOTS, :size])
        seen_trans = jnp.where(last_row, pull_s[...], seen[:SLOTS, size:])
        lefts = as_left(jnp.concatenate([seen_cov, seen[SLOTS:, :size]], axis=0), 1)
        joint = raw(lefts[:two], rows[SLOTS:two], NT)
        cross = joint[:SLOTS] + cross_s[...]
        next_square = joint[SLOTS:] + noise_s[...]
        side = raw(lefts[:SLOTS], rows[two:], NT) + fixed_s[...]
        moved_cov = raw(lefts[two:], rows[two:], NT) + added_ref[ahead]
        moved_trans = seen[two:, size:]

        after_next = (state[4] + state[7], state[5] + state[6])
        after_next = after_next + extent(*after_next)
        new_watch, new_fixed, new_noise = prepare(*after_next)
        linked = link(state[7], next_fixed_s[...], new_watch, new_noise)

        (cross, to_state, to_trans), pivots, quad = eliminate(square, (cross, side, seen_trans))
        scale = jnp.where(last_row, 0.0, lax.rsqrt(pivots))
        tie = cross * scale[:, :SLOTS]
        square_s[...] = (
            next_square
            + jnp.where(last_row, cross, 0.0)
            - raw(as_left(tie, 0), as_right(tie, 0), TN)
        )
        gain, reach = to_state * scale, to_trans * scale
        gain_left, reach_right = as_left(gain, 0), as_right(reach, 0)
        cov_s[...] = moved_cov - raw(gain_left, as_right(gain, 0), TN)
        trans_s[...] = moved_trans - raw(gain_left, reach_right, TN)
        info_s[...] = info_s[...] + raw(as_left(reach, 0), reach_right, TN)
        mean_s[...] = to_state[SLOTS - 1 :, :]
        pull_s[...] = to_trans[SLOTS - 1 :, :]
        watch_s[...], fixed_s[...] = next_watch_s[...], next_fixed_s[...]
        next_watch_s[...], next_fixed_s[...] = new_watch, new_fixed
        carry_s[...], cross_s[...], noise_s[...] = linked

        @pl.when(inside)
        def _():
            counted = jnp.minimum(taken, off_s[0, step + 1] - first)
            logs = jnp.where(iota((SLOTS, size), 0) < counted, jnp.log(pivots), 0.0)
            log_det = jnp.sum(logs, axis=0, keepdims=True)
            squares = jnp.where(iota((1, size), 1) < counted, quad, 0.0)
            squares = jnp.sum(squares, axis=1, keepdims=True)
            count = counted.astype(F32) * LOG_TWO_PI
            kept_lik[mine] = kept_lik[mine] + (log_det + squares + count)

        return state[4:] + after_next

    lax.while_loop(lambda state: state[0] < steps, body, opening + second)

    info, pull = info_s[...], pull_s[...]
    for j in range(own - 1, -1, -1):
        cov = kept_cov[j]
        smooth_cov_ref[j] = cov - dot(dot(cov, info), cov)
        smooth_mean_ref[j : j + 1, :] = kept_mean[j] + dot(pull, cov)
        loglik_ref[:, j : j + 1] = kept_lik[j][:, :1] * (-1.0 / (2.0 * size))
        if j > 0:
            trans = kept_trans[j]
            info = kept_info[j] + dot(dot(trans, info, TN), trans)
            pull = kept_pull[j] + dot(pull, trans)


VMEM = pl.BlockSpec(memory_space=pltpu.VMEM)
LIMIT = 48 * 1024 * 1024


def tables(nw, damping, process_var, obs_var, prior_mean, prior_var):
    size = nw.shape[1]
    return pl.pallas_call(
        tables_kernel,
        out_shape=(
            jax.ShapeDtypeStruct((size, 2 * WINDOW * 3 * size), BF),
            jax.ShapeDtypeStruct((2 * size, (WINDOW - 1) * size), BF),
            jax.ShapeDtypeStruct((WINDOW + 1, size, size), F32),
            jax.ShapeDtypeStruct((8, size), F32),
        ),
        in_specs=[VMEM] * 6,
        out_specs=(VMEM,) * 4,
        compiler_params=pltpu.CompilerParams(vmem_limit_bytes=LIMIT),
        cost_estimate=pl.CostEstimate(flops=10**8, bytes_accessed=2 * 10**6, transcendentals=0),
    )(nw, damping, process_var, obs_var, prior_mean, prior_var)


def chain(position, gathered, strip, big, added, line, own):
    steps, size = gathered.shape[0], gathered.shape[1] // 2
    padded = -(-(steps + WINDOW + 1) // 128) * 128
    square = (size, size)
    return pl.pallas_call(
        functools.partial(chain_kernel, own),
        out_shape=(
            jax.ShapeDtypeStruct((own, size), F32),
            jax.ShapeDtypeStruct((own, size, size), F32),
            jax.ShapeDtypeStruct((1, own), F32),
        ),
        in_specs=[pl.BlockSpec(memory_space=pltpu.SMEM)] + [VMEM] * 5,
        out_specs=(VMEM,) * 3,
        scratch_shapes=[
            pltpu.VMEM((padded, size), F32),
            pltpu.VMEM((padded, size), F32),
            pltpu.VMEM((padded, size), jnp.int32),
            pltpu.VMEM((8, padded), jnp.int32),
            pltpu.SMEM((8, padded), jnp.int32),
            pltpu.VMEM((SLOTS, 3 * size), BF),
            pltpu.VMEM((SLOTS, size), F32),
            pltpu.VMEM((SLOTS, SLOTS), F32),
            pltpu.VMEM((SLOTS, 3 * size), BF),
            pltpu.VMEM((SLOTS, SLOTS), F32),
            pltpu.VMEM((SLOTS, SLOTS), F32),
            pltpu.VMEM((SLOTS, 3 * size), BF),
            pltpu.VMEM((SLOTS, size), F32),
            pltpu.VMEM(square, F32),
            pltpu.VMEM(square, F32),
            pltpu.VMEM(square, F32),
            pltpu.VMEM((1, size), F32),
            pltpu.VMEM((1, size), F32),
            pltpu.VMEM((own,) + square, F32),
            pltpu.VMEM((own, 1, size), F32),
            pltpu.VMEM((own,) + square, F32),
            pltpu.VMEM((own,) + square, F32),
            pltpu.VMEM((own, 1, size), F32),
            pltpu.VMEM((own, 1, size), F32),
            pltpu.SemaphoreType.DMA(()),
        ],
        compiler_params=pltpu.CompilerParams(vmem_limit_bytes=LIMIT),
    )(position, gathered, strip, big, added, line)


def gather_all(block, axis):
    size = lax.axis_size(axis)
    held, reach = block, 1
    if size & (size - 1):
        return lax.all_gather(block, axis, tiled=True), jnp.int32(0)
    while reach < size:
        pairs = [(i, i ^ reach) for i in range(size)]
        held = jnp.concatenate([held, lax.ppermute(held, axis, pairs)], axis=0)
        reach *= 2
    return held, lax.axis_index(axis).astype(jnp.int32)


def local(
    observed, obs_mask, prior_mean, prior_var, neighbor_weights, damping, process_var, obs_var
):
    own = observed.shape[0]
    block = jnp.concatenate([observed, obs_mask.astype(F32)], axis=1)
    gathered, flip = gather_all(block, "tm")
    position = jnp.stack([lax.axis_index("tm").astype(jnp.int32), flip])
    made = tables(
        neighbor_weights, damping[None], process_var[None], obs_var[None], prior_mean[None], prior_var[None]
    )
    smooth_mean, smooth_cov, loglik = chain(position, gathered, *made, own)
    return smooth_mean, smooth_cov, loglik.reshape(own)


def solution(mesh):
    return jax.shard_map(
        local,
        mesh=mesh,
        in_specs=(
            P(("parts", "tm"), None),
            P(("parts", "tm"), None),
            P("parts"),
            P("parts"),
            P(),
            P(),
            P(),
            P(),
        ),
        out_specs=(P(("parts", "tm"), None), P(("parts", "tm"), None, None), P(("parts", "tm"))),
        check_vma=False,
    )
```

```python
import functools
import math

import jax
import jax.numpy as jnp
from jax import lax
from jax.experimental import pallas as pl
from jax.experimental.pallas import tpu as pltpu
from jax.sharding import PartitionSpec as P

GX = 16
GY = 8
OFFSETS = ((-1, -1), (-1, 0), (-1, 1), (0, -1), (0, 1), (1, -1), (1, 0), (1, 1))
LOG_TWO_PI = math.log(2.0 * math.pi)

WINDOW = 5
SLOTS = 32
FAR = 1 << 29

NN = (((1,), (0,)), ((), ()))
NT = (((1,), (1,)), ((), ()))
TN = (((0,), (0,)), ((), ()))
BF = jnp.bfloat16
F32 = jnp.float32


def halves(x):
    high = x.astype(BF)
    return high, (x - high.astype(F32)).astype(BF)


def as_left(x, axis):
    high, low = halves(x)
    return jnp.concatenate([high, high, low], axis=axis)


def as_right(x, axis):
    high, low = halves(x)
    return jnp.concatenate([high, low, high], axis=axis)


def raw(left, right, dims):
    return lax.dot_general(left, right, dims, preferred_element_type=F32)


def dot(left, right, dims=NN):
    (left_axis,), (right_axis,) = dims[0]
    return raw(as_left(left, left_axis), as_right(right, right_axis), dims)


def iota(shape, axis):
    return lax.broadcasted_iota(jnp.int32, shape, axis)


def transition(nw, damping):
    size = GX * GY
    source, cell = iota((size, size), 0), iota((size, size), 1)
    row, column = cell // GY, cell % GY
    source_row, source_column = source // GY, source % GY
    centre = 1.0 - jnp.sum(nw, axis=0, keepdims=True) - damping
    flipped = jnp.where(source == cell, centre, 0.0)
    for index, (dx, dy) in enumerate(OFFSETS):
        hit = (source_row == row + dx) & (source_column == column + dy)
        flipped = flipped + jnp.where(hit, nw[index : index + 1, :], 0.0)
    return jnp.transpose(flipped)


def eliminate(square, sides):
    tiles = SLOTS // 8
    rows, lanes = iota((8, 128), 0), iota((8, 128), 1)
    columns = {}
    for k in range(SLOTS - 1):
        for tile in range(k // 8, tiles):
            block = square[8 * tile : 8 * tile + 8, k : k + 1]
            columns[k, tile] = jnp.broadcast_to(block, (8, 128))
    parts = [[side[8 * t : 8 * t + 8, :] for t in range(tiles)] for side in sides]
    pivots = [jnp.ones((8, 128), F32) for _ in range(tiles)]
    quad = jnp.zeros((8, 128), F32)

    def spread(block, row):
        return jnp.broadcast_to(block[row : row + 1, :], (8, 128))

    for j in range(SLOTS - 1):
        home, row = divmod(j, 8)
        pivot = spread(columns[j, home], row)
        pivots[home] = jnp.where(rows == row, pivot, pivots[home])
        inverse = 1.0 / pivot
        weights = {}
        for tile in range(home, tiles):
            scaled = columns[j, tile] * inverse
            if tile == home:
                scaled = jnp.where(rows > row, scaled, 0.0)
            weights[tile] = scaled
        quad = jnp.where(lanes == j, weights[tiles - 1] * columns[j, tiles - 1], quad)
        for k in range(j + 1, SLOTS - 1):
            across = spread(columns[k, k // 8], row) if k // 8 == home else None
            if across is None:
                across = spread(columns[j, k // 8], k % 8)
            for tile in range(k // 8, tiles):
                columns[k, tile] = columns[k, tile] - weights[tile] * across
        for part in parts:
            across = jnp.broadcast_to(part[home][row : row + 1, :], part[home].shape)
            for tile in range(home, tiles):
                part[tile] = part[tile] - weights[tile][:, : part[tile].shape[1]] * across
    pivots = jnp.concatenate(pivots, axis=0)
    sides = [jnp.concatenate(part, axis=0) for part in parts]
    return sides, pivots, quad[7:8, :]


def tables_kernel(
    nw_ref, damping_ref, process_ref, noise_ref, mean_ref, var_ref, strip_ref, big_ref, added_ref, line_ref
):
    size = GX * GY
    process = process_ref[...]
    line_ref[...] = jnp.concatenate(
        [mean_ref[...], var_ref[...], process, noise_ref[...], jnp.zeros((4, size), F32)], axis=0
    )
    powers = [
        (iota((size, size), 0) == iota((size, size), 1)).astype(F32),
        transition(nw_ref[...], damping_ref[...]),
    ]
    for e in range(2, WINDOW + 1):
        powers.append(dot(powers[(e + 1) // 2], powers[e // 2]))
    band = 3 * size
    strip_ref[...] = jnp.zeros_like(strip_ref)
    for e in range(WINDOW + 1):
        at = (WINDOW - e) * band
        strip_ref[:, at : at + band] = as_right(powers[e], 1)
    added_ref[0] = jnp.zeros((size, size), F32)
    added = jnp.zeros((size, size), F32)
    for e in range(1, WINDOW + 1):
        added = added + dot(powers[e - 1] * process, powers[e - 1], NT)
        added_ref[e] = added
    for i in range(1, WINDOW):
        high, low = halves(powers[i])
        big_ref[:size, (i - 1) * size : i * size] = high
        big_ref[size:, (i - 1) * size : i * size] = low


def chain_kernel(
    own,
    position_ref,
    gathered_ref,
    strip_ref,
    big_ref,
    added_ref,
    line_ref,
    smooth_mean_ref,
    smooth_cov_ref,
    loglik_ref,
    mask_s,
    obs_s,
    rank_s,
    off_v,
    off_s,
    watch_s,
    fixed_s,
    square_s,
    carry_s,
    cross_s,
    noise_s,
    next_watch_s,
    next_fixed_s,
    cov_s,
    trans_s,
    info_s,
    mean_s,
    pull_s,
    kept_cov,
    kept_mean,
    kept_trans,
    kept_info,
    kept_pull,
    kept_lik,
    sem,
):
    size = GX * GY
    steps = gathered_ref.shape[0]
    padded = mask_s.shape[0]
    position = position_ref[0]
    base = position * own
    process, noise = line_ref[2:3, :], line_ref[3:4, :]

    mask_s[...] = jnp.zeros_like(mask_s)
    obs_s[...] = jnp.zeros_like(obs_s)
    for block in range(steps // own):
        held = (position_ref[1] ^ block) * own
        for row in range(own):
            at = block * own + row
            line = gathered_ref[pl.ds(held + row, 1), :]
            obs_s[at : at + 1, :] = line[:, :size]
            mask_s[at : at + 1, :] = line[:, size:]
    mask = mask_s[...]
    mask_b = mask.astype(BF)
    before = (iota((padded, padded), 0) < iota((padded, padded), 1)).astype(BF)
    after = (iota((padded, padded), 0) > iota((padded, padded), 1)).astype(BF)
    counts_row = raw(jnp.ones((8, size), BF), mask_b, NT)
    off_v[...] = raw(counts_row.astype(BF), before, NN).astype(jnp.int32)
    copy = pltpu.make_async_copy(off_v, off_s, sem)
    copy.start()
    counts = raw(mask_b, jnp.ones((size, size), BF), NN)
    within = (iota((size, size), 0) < iota((size, size), 1)).astype(BF)
    rank = raw(mask_b, within, NN) + raw(after, counts.astype(BF), NN)
    rank_s[...] = jnp.where(mask > 0.0, rank.astype(jnp.int32), FAR)

    eye = (iota((size, size), 0) == iota((size, size), 1)).astype(F32)
    band = 3 * size
    cov_s[...] = eye * line_ref[1:2, :]
    mean_s[...] = line_ref[0:1, :]
    trans_s[...] = jnp.zeros_like(trans_s)
    info_s[...] = jnp.zeros_like(info_s)
    pull_s[...] = jnp.zeros_like(pull_s)
    kept_lik[...] = jnp.zeros_like(kept_lik)
    copy.wait()
    last_row = iota((SLOTS, 1), 0) == SLOTS - 1

    def is_own(step):
        return (step >= base) & (step < base + own)

    def extent(step, first):
        last = base + own - 1
        cut = jnp.where(step < base, base, jnp.where(step < last, step + 1, steps))
        end = jnp.minimum(step + WINDOW, cut)
        taken = jnp.minimum(off_s[0, end] - first, SLOTS - 1)
        ahead = jnp.int32(0)
        for i in range(1, WINDOW + 1):
            done = (step + i <= end) & (off_s[0, step + i] <= first + taken)
            ahead = ahead + done.astype(jnp.int32)
        return taken, ahead

    def power(e, count=1):
        return strip_ref[:, pl.ds(pl.multiple_of((WINDOW - e) * band, band), count * band)]

    def prepare(step, first, taken, ahead):
        slot = iota((SLOTS, size), 0)
        picks = []
        for i in range(WINDOW):
            where = rank_s[pl.ds(step + i, 1), :] - first
            picks.append(jnp.where((slot == where) & (slot < taken), 1.0, 0.0))
        tail = jnp.concatenate(picks[1:], axis=0).astype(BF)
        rows = raw(jnp.concatenate([tail, tail], axis=1), big_ref[...], NN)

        def moved_pick(i, e):
            if e == 0:
                return picks[i]
            return rows[(i - 1) * SLOTS : i * SLOTS, (e - 1) * size : e * size]

        watch = as_right(sum(moved_pick(i, i) for i in range(WINDOW)), 1)
        lefts, rights = [], []
        for l in range(1, WINDOW):
            shock = sum(moved_pick(i, i - l) for i in range(l, WINDOW))
            lefts.append(as_left(shock * process, 1))
            rights.append(as_right(shock, 1))
        lefts = jnp.concatenate(lefts, axis=1)
        noise_part = raw(lefts, jnp.concatenate(rights, axis=1), NT)
        side_part = raw(lefts, power(ahead - 1, WINDOW - 1), NT)
        readings = sum(picks[i] * obs_s[pl.ds(step + i, 1), :] for i in range(WINDOW))
        readings = jnp.sum(readings, axis=1, keepdims=True)
        variances = jnp.sum(sum(picks) * noise, axis=1, keepdims=True)
        variances = variances + (iota((SLOTS, 1), 0) >= taken).astype(F32)
        diagonal = iota((SLOTS, SLOTS), 0) == iota((SLOTS, SLOTS), 1)
        across = jnp.sum(jnp.where(diagonal, readings, 0.0), axis=0, keepdims=True)
        own_noise = jnp.where(diagonal, variances, 0.0) - jnp.where(last_row, across, 0.0)
        return watch, side_part, noise_part + own_noise

    def link(ahead, fixed, watch, noise):
        at = pl.multiple_of((WINDOW - ahead) * band, band)
        high, low = strip_ref[:, pl.ds(at, size)], strip_ref[:, pl.ds(at + size, size)]
        rights = [jnp.concatenate([high, high, low], axis=0), as_left(added_ref[ahead], 0)]
        onward = raw(watch, jnp.concatenate(rights, axis=1), NN)
        both = raw(as_left(jnp.concatenate([fixed, onward[:, size:]], axis=0), 1), watch, NT)
        return as_right(onward[:, :size], 1), both[:SLOTS], noise + both[SLOTS:]

    zero = jnp.int32(0)
    opening = (zero, zero) + extent(zero, zero)
    second = (opening[3], opening[2])
    second = second + extent(*second)
    watch, fixed, noise_now = prepare(*opening)
    seen = jnp.where(last_row, mean_s[...], raw(watch, as_left(cov_s[...], 0), NN))
    square_s[...] = raw(as_left(seen, 1), watch, NT) + noise_now
    watch_s[...], fixed_s[...] = watch, fixed
    watch, next_fixed, noise_now = prepare(*second)
    next_watch_s[...], next_fixed_s[...] = watch, next_fixed
    carry_s[...], cross_s[...], noise_s[...] = link(opening[3], fixed, watch, noise_now)

    def body(state):
        step, first, taken, ahead = state[:4]
        inside = is_own(step)
        mine = jnp.clip(step - base, 0, own - 1)

        @pl.when(inside & (first == off_s[0, step]))
        def _():
            kept_cov[mine] = cov_s[...]
            kept_mean[mine] = mean_s[...]
            kept_trans[mine] = trans_s[...]
            kept_info[mine] = info_s[...]
            kept_pull[mine] = pull_s[...]
            trans_s[...] = eye
            info_s[...] = jnp.zeros_like(info_s)
            pull_s[...] = jnp.zeros_like(pull_s)

        square = square_s[...]
        two = 2 * SLOTS
        rows = jnp.concatenate([watch_s[...], carry_s[...], power(ahead)], axis=0)
        seen = raw(rows, as_left(jnp.concatenate([cov_s[...], trans_s[...]], axis=1), 0), NN)
        seen_cov = jnp.where(last_row, mean_s[...], seen[:SLOTS, :size])
        seen_trans = jnp.where(last_row, pull_s[...], seen[:SLOTS, size:])
        lefts = as_left(jnp.concatenate([seen_cov, seen[SLOTS:, :size]], axis=0), 1)
        joint = raw(lefts[:two], rows[SLOTS:two], NT)
        cross = joint[:SLOTS] + cross_s[...]
        next_square = joint[SLOTS:] + noise_s[...]
        side = raw(lefts[:SLOTS], rows[two:], NT) + fixed_s[...]
        moved_cov = raw(lefts[two:], rows[two:], NT) + added_ref[ahead]
        moved_trans = seen[two:, size:]

        after_next = (state[4] + state[7], state[5] + state[6])
        after_next = after_next + extent(*after_next)
        new_watch, new_fixed, new_noise = prepare(*after_next)
        linked = link(state[7], next_fixed_s[...], new_watch, new_noise)

        (cross, to_state, to_trans), pivots, quad = eliminate(square, (cross, side, seen_trans))
        scale = jnp.where(last_row, 0.0, lax.rsqrt(pivots))
        tie = cross * scale[:, :SLOTS]
        square_s[...] = (
            next_square
            + jnp.where(last_row, cross, 0.0)
            - raw(as_left(tie, 0), as_right(tie, 0), TN)
        )
        gain, reach = to_state * scale, to_trans * scale
        gain_left, reach_right = as_left(gain, 0), as_right(reach, 0)
        cov_s[...] = moved_cov - raw(gain_left, as_right(gain, 0), TN)
        trans_s[...] = moved_trans - raw(gain_left, reach_right, TN)
        info_s[...] = info_s[...] + raw(as_left(reach, 0), reach_right, TN)
        mean_s[...] = to_state[SLOTS - 1 :, :]
        pull_s[...] = to_trans[SLOTS - 1 :, :]
        watch_s[...], fixed_s[...] = next_watch_s[...], next_fixed_s[...]
        next_watch_s[...], next_fixed_s[...] = new_watch, new_fixed
        carry_s[...], cross_s[...], noise_s[...] = linked

        @pl.when(inside)
        def _():
            counted = jnp.minimum(taken, off_s[0, step + 1] - first)
            logs = jnp.where(iota((SLOTS, size), 0) < counted, jnp.log(pivots), 0.0)
            log_det = jnp.sum(logs, axis=0, keepdims=True)
            squares = jnp.where(iota((1, size), 1) < counted, quad, 0.0)
            squares = jnp.sum(squares, axis=1, keepdims=True)
            count = counted.astype(F32) * LOG_TWO_PI
            kept_lik[mine] = kept_lik[mine] + (log_det + squares + count)

        return state[4:] + after_next

    lax.while_loop(lambda state: state[0] < steps, body, opening + second)

    info, pull = info_s[...], pull_s[...]
    for j in range(own - 1, -1, -1):
        cov = kept_cov[j]
        smooth_cov_ref[j] = cov - dot(dot(cov, info), cov)
        smooth_mean_ref[j : j + 1, :] = kept_mean[j] + dot(pull, cov)
        loglik_ref[:, j : j + 1] = kept_lik[j][:, :1] * (-1.0 / (2.0 * size))
        if j > 0:
            trans = kept_trans[j]
            info = kept_info[j] + dot(dot(trans, info, TN), trans)
            pull = kept_pull[j] + dot(pull, trans)


VMEM = pl.BlockSpec(memory_space=pltpu.VMEM)
LIMIT = 48 * 1024 * 1024


def tables(nw, damping, process_var, obs_var, prior_mean, prior_var):
    size = nw.shape[1]
    return pl.pallas_call(
        tables_kernel,
        out_shape=(
            jax.ShapeDtypeStruct((size, 2 * WINDOW * 3 * size), BF),
            jax.ShapeDtypeStruct((2 * size, (WINDOW - 1) * size), BF),
            jax.ShapeDtypeStruct((WINDOW + 1, size, size), F32),
            jax.ShapeDtypeStruct((8, size), F32),
        ),
        in_specs=[VMEM] * 6,
        out_specs=(VMEM,) * 4,
        compiler_params=pltpu.CompilerParams(vmem_limit_bytes=LIMIT),
        cost_estimate=pl.CostEstimate(flops=10**8, bytes_accessed=2 * 10**6, transcendentals=0),
    )(nw, damping, process_var, obs_var, prior_mean, prior_var)


def chain(position, gathered, strip, big, added, line, own):
    steps, size = gathered.shape[0], gathered.shape[1] // 2
    padded = -(-(steps + WINDOW + 1) // 128) * 128
    square = (size, size)
    return pl.pallas_call(
        functools.partial(chain_kernel, own),
        out_shape=(
            jax.ShapeDtypeStruct((own, size), F32),
            jax.ShapeDtypeStruct((own, size, size), F32),
            jax.ShapeDtypeStruct((1, own), F32),
        ),
        in_specs=[pl.BlockSpec(memory_space=pltpu.SMEM)] + [VMEM] * 5,
        out_specs=(VMEM,) * 3,
        scratch_shapes=[
            pltpu.VMEM((padded, size), F32),
            pltpu.VMEM((padded, size), F32),
            pltpu.VMEM((padded, size), jnp.int32),
            pltpu.VMEM((8, padded), jnp.int32),
            pltpu.SMEM((8, padded), jnp.int32),
            pltpu.VMEM((SLOTS, 3 * size), BF),
            pltpu.VMEM((SLOTS, size), F32),
            pltpu.VMEM((SLOTS, SLOTS), F32),
            pltpu.VMEM((SLOTS, 3 * size), BF),
            pltpu.VMEM((SLOTS, SLOTS), F32),
            pltpu.VMEM((SLOTS, SLOTS), F32),
            pltpu.VMEM((SLOTS, 3 * size), BF),
            pltpu.VMEM((SLOTS, size), F32),
            pltpu.VMEM(square, F32),
            pltpu.VMEM(square, F32),
            pltpu.VMEM(square, F32),
            pltpu.VMEM((1, size), F32),
            pltpu.VMEM((1, size), F32),
            pltpu.VMEM((own,) + square, F32),
            pltpu.VMEM((own, 1, size), F32),
            pltpu.VMEM((own,) + square, F32),
            pltpu.VMEM((own,) + square, F32),
            pltpu.VMEM((own, 1, size), F32),
            pltpu.VMEM((own, 1, size), F32),
            pltpu.SemaphoreType.DMA(()),
        ],
        compiler_params=pltpu.CompilerParams(vmem_limit_bytes=LIMIT),
    )(position, gathered, strip, big, added, line)


def gather_all(observed, obs_mask, axis):
    size = lax.axis_size(axis)

    def joined(*pieces):
        masks = [mask.astype(F32) for mask in pieces[1::2]]
        return jnp.concatenate(
            [jnp.concatenate(pieces[::2], axis=0), jnp.concatenate(masks, axis=0)], axis=1
        )

    def across(array, reach):
        return lax.ppermute(array, axis, [(i, i ^ reach) for i in range(size)])

    if size == 1 or size & (size - 1):
        return lax.all_gather(joined(observed, obs_mask), axis, tiled=True), jnp.int32(0)
    held = joined(observed, obs_mask, across(observed, 1), across(obs_mask, 1))
    reach = 2
    while reach < size:
        held = jnp.concatenate([held, across(held, reach)], axis=0)
        reach *= 2
    return held, lax.axis_index(axis).astype(jnp.int32)


def local(
    observed, obs_mask, prior_mean, prior_var, neighbor_weights, damping, process_var, obs_var
):
    own = observed.shape[0]
    gathered, flip = gather_all(observed, obs_mask, "tm")
    position = jnp.stack([lax.axis_index("tm").astype(jnp.int32), flip])
    made = tables(
        neighbor_weights, damping[None], process_var[None], obs_var[None], prior_mean[None], prior_var[None]
    )
    smooth_mean, smooth_cov, loglik = chain(position, gathered, *made, own)
    return smooth_mean, smooth_cov, loglik.reshape(own)


def solution(mesh):
    return jax.shard_map(
        local,
        mesh=mesh,
        in_specs=(
            P(("parts", "tm"), None),
            P(("parts", "tm"), None),
            P("parts"),
            P("parts"),
            P(),
            P(),
            P(),
            P(),
        ),
        out_specs=(P(("parts", "tm"), None), P(("parts", "tm"), None, None), P(("parts", "tm"))),
        check_vma=False,
    )
```

```python
import functools
import math

import jax
import jax.numpy as jnp
from jax import lax
from jax.experimental import pallas as pl
from jax.experimental.pallas import tpu as pltpu
from jax.sharding import PartitionSpec as P

GX = 16
GY = 8
OFFSETS = ((-1, -1), (-1, 0), (-1, 1), (0, -1), (0, 1), (1, -1), (1, 0), (1, 1))
LOG_TWO_PI = math.log(2.0 * math.pi)

WINDOW = 4
SLOTS = 32
FAR = 1 << 29

NN = (((1,), (0,)), ((), ()))
NT = (((1,), (1,)), ((), ()))
TN = (((0,), (0,)), ((), ()))
BF = jnp.bfloat16
F32 = jnp.float32


def halves(x):
    high = x.astype(BF)
    return high, (x - high.astype(F32)).astype(BF)


def as_left(x, axis):
    high, low = halves(x)
    return jnp.concatenate([high, high, low], axis=axis)


def as_right(x, axis):
    high, low = halves(x)
    return jnp.concatenate([high, low, high], axis=axis)


def raw(left, right, dims):
    return lax.dot_general(left, right, dims, preferred_element_type=F32)


def dot(left, right, dims=NN):
    (left_axis,), (right_axis,) = dims[0]
    return raw(as_left(left, left_axis), as_right(right, right_axis), dims)


def iota(shape, axis):
    return lax.broadcasted_iota(jnp.int32, shape, axis)


def transition(nw, damping):
    size = GX * GY
    source, cell = iota((size, size), 0), iota((size, size), 1)
    row, column = cell // GY, cell % GY
    source_row, source_column = source // GY, source % GY
    centre = 1.0 - jnp.sum(nw, axis=0, keepdims=True) - damping
    flipped = jnp.where(source == cell, centre, 0.0)
    for index, (dx, dy) in enumerate(OFFSETS):
        hit = (source_row == row + dx) & (source_column == column + dy)
        flipped = flipped + jnp.where(hit, nw[index : index + 1, :], 0.0)
    return jnp.transpose(flipped)


def eliminate(square, sides):
    tiles = SLOTS // 8
    rows, lanes = iota((8, 128), 0), iota((8, 128), 1)
    columns = {}
    for k in range(SLOTS - 1):
        for tile in range(k // 8, tiles):
            block = square[8 * tile : 8 * tile + 8, k : k + 1]
            columns[k, tile] = jnp.broadcast_to(block, (8, 128))
    parts = [[side[8 * t : 8 * t + 8, :] for t in range(tiles)] for side in sides]
    pivots = [jnp.ones((8, 128), F32) for _ in range(tiles)]
    quad = jnp.zeros((8, 128), F32)

    def spread(block, row):
        return jnp.broadcast_to(block[row : row + 1, :], (8, 128))

    for j in range(SLOTS - 1):
        home, row = divmod(j, 8)
        pivot = spread(columns[j, home], row)
        pivots[home] = jnp.where(rows == row, pivot, pivots[home])
        inverse = 1.0 / pivot
        weights = {}
        for tile in range(home, tiles):
            scaled = columns[j, tile] * inverse
            if tile == home:
                scaled = jnp.where(rows > row, scaled, 0.0)
            weights[tile] = scaled
        quad = jnp.where(lanes == j, weights[tiles - 1] * columns[j, tiles - 1], quad)
        for k in range(j + 1, SLOTS - 1):
            across = spread(columns[k, k // 8], row) if k // 8 == home else None
            if across is None:
                across = spread(columns[j, k // 8], k % 8)
            for tile in range(k // 8, tiles):
                columns[k, tile] = columns[k, tile] - weights[tile] * across
        for part in parts:
            across = jnp.broadcast_to(part[home][row : row + 1, :], part[home].shape)
            for tile in range(home, tiles):
                part[tile] = part[tile] - weights[tile][:, : part[tile].shape[1]] * across
    pivots = jnp.concatenate(pivots, axis=0)
    sides = [jnp.concatenate(part, axis=0) for part in parts]
    return sides, pivots, quad[7:8, :]


def tables_kernel(
    nw_ref, damping_ref, process_ref, noise_ref, mean_ref, var_ref, strip_ref, big_ref, added_ref, line_ref
):
    size = GX * GY
    process = process_ref[...]
    line_ref[...] = jnp.concatenate(
        [mean_ref[...], var_ref[...], process, noise_ref[...], jnp.zeros((4, size), F32)], axis=0
    )
    powers = [
        (iota((size, size), 0) == iota((size, size), 1)).astype(F32),
        transition(nw_ref[...], damping_ref[...]),
    ]
    for e in range(2, WINDOW + 1):
        powers.append(dot(powers[(e + 1) // 2], powers[e // 2]))
    band = 3 * size
    strip_ref[...] = jnp.zeros_like(strip_ref)
    for e in range(WINDOW + 1):
        at = (WINDOW - e) * band
        strip_ref[:, at : at + band] = as_right(powers[e], 1)
    added_ref[0] = jnp.zeros((size, size), F32)
    added = jnp.zeros((size, size), F32)
    for e in range(1, WINDOW + 1):
        added = added + dot(powers[e - 1] * process, powers[e - 1], NT)
        added_ref[e] = added
    for i in range(1, WINDOW):
        high, low = halves(powers[i])
        big_ref[:size, (i - 1) * size : i * size] = high
        big_ref[size:, (i - 1) * size : i * size] = low


def chain_kernel(
    own,
    position_ref,
    gathered_ref,
    strip_ref,
    big_ref,
    added_ref,
    line_ref,
    smooth_mean_ref,
    smooth_cov_ref,
    loglik_ref,
    mask_s,
    obs_s,
    rank_s,
    off_v,
    off_s,
    watch_s,
    fixed_s,
    square_s,
    carry_s,
    cross_s,
    noise_s,
    next_watch_s,
    next_fixed_s,
    cov_s,
    trans_s,
    info_s,
    mean_s,
    pull_s,
    kept_cov,
    kept_mean,
    kept_trans,
    kept_info,
    kept_pull,
    kept_lik,
    sem,
):
    size = GX * GY
    steps = gathered_ref.shape[0]
    padded = mask_s.shape[0]
    position = position_ref[0]
    base = position * own
    process, noise = line_ref[2:3, :], line_ref[3:4, :]

    mask_s[...] = jnp.zeros_like(mask_s)
    obs_s[...] = jnp.zeros_like(obs_s)
    for block in range(steps // own):
        held = (position_ref[1] ^ block) * own
        for row in range(own):
            at = block * own + row
            line = gathered_ref[pl.ds(held + row, 1), :]
            obs_s[at : at + 1, :] = line[:, :size]
            mask_s[at : at + 1, :] = line[:, size:]
    mask = mask_s[...]
    mask_b = mask.astype(BF)
    before = (iota((padded, padded), 0) < iota((padded, padded), 1)).astype(BF)
    after = (iota((padded, padded), 0) > iota((padded, padded), 1)).astype(BF)
    counts_row = raw(jnp.ones((8, size), BF), mask_b, NT)
    off_v[...] = raw(counts_row.astype(BF), before, NN).astype(jnp.int32)
    copy = pltpu.make_async_copy(off_v, off_s, sem)
    copy.start()
    counts = raw(mask_b, jnp.ones((size, size), BF), NN)
    within = (iota((size, size), 0) < iota((size, size), 1)).astype(BF)
    rank = raw(mask_b, within, NN) + raw(after, counts.astype(BF), NN)
    rank_s[...] = jnp.where(mask > 0.0, rank.astype(jnp.int32), FAR)

    eye = (iota((size, size), 0) == iota((size, size), 1)).astype(F32)
    band = 3 * size
    cov_s[...] = eye * line_ref[1:2, :]
    mean_s[...] = line_ref[0:1, :]
    trans_s[...] = jnp.zeros_like(trans_s)
    info_s[...] = jnp.zeros_like(info_s)
    pull_s[...] = jnp.zeros_like(pull_s)
    kept_lik[...] = jnp.zeros_like(kept_lik)
    copy.wait()
    last_row = iota((SLOTS, 1), 0) == SLOTS - 1

    def is_own(step):
        return (step >= base) & (step < base + own)

    def extent(step, first):
        last = base + own - 1
        cut = jnp.where(step < base, base, jnp.where(step < last, step + 1, steps))
        end = jnp.minimum(step + WINDOW, cut)
        taken = jnp.minimum(off_s[0, end] - first, SLOTS - 1)
        ahead = jnp.int32(0)
        for i in range(1, WINDOW + 1):
            done = (step + i <= end) & (off_s[0, step + i] <= first + taken)
            ahead = ahead + done.astype(jnp.int32)
        return taken, ahead

    def power(e, count=1):
        return strip_ref[:, pl.ds(pl.multiple_of((WINDOW - e) * band, band), count * band)]

    def prepare(step, first, taken, ahead):
        slot = iota((SLOTS, size), 0)
        picks = []
        for i in range(WINDOW):
            where = rank_s[pl.ds(step + i, 1), :] - first
            picks.append(jnp.where((slot == where) & (slot < taken), 1.0, 0.0))
        tail = jnp.concatenate(picks[1:], axis=0).astype(BF)
        rows = raw(jnp.concatenate([tail, tail], axis=1), big_ref[...], NN)

        def moved_pick(i, e):
            if e == 0:
                return picks[i]
            return rows[(i - 1) * SLOTS : i * SLOTS, (e - 1) * size : e * size]

        watch = as_right(sum(moved_pick(i, i) for i in range(WINDOW)), 1)
        lefts, rights = [], []
        for l in range(1, WINDOW):
            shock = sum(moved_pick(i, i - l) for i in range(l, WINDOW))
            lefts.append(as_left(shock * process, 1))
            rights.append(as_right(shock, 1))
        lefts = jnp.concatenate(lefts, axis=1)
        noise_part = raw(lefts, jnp.concatenate(rights, axis=1), NT)
        side_part = raw(lefts, power(ahead - 1, WINDOW - 1), NT)
        readings = sum(picks[i] * obs_s[pl.ds(step + i, 1), :] for i in range(WINDOW))
        readings = jnp.sum(readings, axis=1, keepdims=True)
        variances = jnp.sum(sum(picks) * noise, axis=1, keepdims=True)
        variances = variances + (iota((SLOTS, 1), 0) >= taken).astype(F32)
        diagonal = iota((SLOTS, SLOTS), 0) == iota((SLOTS, SLOTS), 1)
        across = jnp.sum(jnp.where(diagonal, readings, 0.0), axis=0, keepdims=True)
        own_noise = jnp.where(diagonal, variances, 0.0) - jnp.where(last_row, across, 0.0)
        return watch, side_part, noise_part + own_noise

    def link(ahead, fixed, watch, noise):
        at = pl.multiple_of((WINDOW - ahead) * band, band)
        high, low = strip_ref[:, pl.ds(at, size)], strip_ref[:, pl.ds(at + size, size)]
        rights = [jnp.concatenate([high, high, low], axis=0), as_left(added_ref[ahead], 0)]
        onward = raw(watch, jnp.concatenate(rights, axis=1), NN)
        both = raw(as_left(jnp.concatenate([fixed, onward[:, size:]], axis=0), 1), watch, NT)
        return as_right(onward[:, :size], 1), both[:SLOTS], noise + both[SLOTS:]

    zero = jnp.int32(0)
    opening = (zero, zero) + extent(zero, zero)
    second = (opening[3], opening[2])
    second = second + extent(*second)
    watch, fixed, noise_now = prepare(*opening)
    seen = jnp.where(last_row, mean_s[...], raw(watch, as_left(cov_s[...], 0), NN))
    square_s[...] = raw(as_left(seen, 1), watch, NT) + noise_now
    watch_s[...], fixed_s[...] = watch, fixed
    watch, next_fixed, noise_now = prepare(*second)
    next_watch_s[...], next_fixed_s[...] = watch, next_fixed
    carry_s[...], cross_s[...], noise_s[...] = link(opening[3], fixed, watch, noise_now)

    def body(state):
        step, first, taken, ahead = state[:4]
        inside = is_own(step)
        mine = jnp.clip(step - base, 0, own - 1)

        @pl.when(inside & (first == off_s[0, step]))
        def _():
            kept_cov[mine] = cov_s[...]
            kept_mean[mine] = mean_s[...]
            kept_trans[mine] = trans_s[...]
            kept_info[mine] = info_s[...]
            kept_pull[mine] = pull_s[...]
            trans_s[...] = eye
            info_s[...] = jnp.zeros_like(info_s)
            pull_s[...] = jnp.zeros_like(pull_s)

        square = square_s[...]
        two = 2 * SLOTS
        rows = jnp.concatenate([watch_s[...], carry_s[...], power(ahead)], axis=0)
        seen = raw(rows, as_left(jnp.concatenate([cov_s[...], trans_s[...]], axis=1), 0), NN)
        seen_cov = jnp.where(last_row, mean_s[...], seen[:SLOTS, :size])
        seen_trans = jnp.where(last_row, pull_s[...], seen[:SLOTS, size:])
        lefts = as_left(jnp.concatenate([seen_cov, seen[SLOTS:, :size]], axis=0), 1)
        joint = raw(lefts[:two], rows[SLOTS:two], NT)
        cross = joint[:SLOTS] + cross_s[...]
        next_square = joint[SLOTS:] + noise_s[...]
        side = raw(lefts[:SLOTS], rows[two:], NT) + fixed_s[...]
        moved_cov = raw(lefts[two:], rows[two:], NT) + added_ref[ahead]
        moved_trans = seen[two:, size:]

        after_next = (state[4] + state[7], state[5] + state[6])
        after_next = after_next + extent(*after_next)
        new_watch, new_fixed, new_noise = prepare(*after_next)
        linked = link(state[7], next_fixed_s[...], new_watch, new_noise)

        (cross, to_state, to_trans), pivots, quad = eliminate(square, (cross, side, seen_trans))
        scale = jnp.where(last_row, 0.0, lax.rsqrt(pivots))
        tie = cross * scale[:, :SLOTS]
        square_s[...] = (
            next_square
            + jnp.where(last_row, cross, 0.0)
            - raw(as_left(tie, 0), as_right(tie, 0), TN)
        )
        gain, reach = to_state * scale, to_trans * scale
        gain_left, reach_right = as_left(gain, 0), as_right(reach, 0)
        cov_s[...] = moved_cov - raw(gain_left, as_right(gain, 0), TN)
        trans_s[...] = moved_trans - raw(gain_left, reach_right, TN)
        info_s[...] = info_s[...] + raw(as_left(reach, 0), reach_right, TN)
        mean_s[...] = to_state[SLOTS - 1 :, :]
        pull_s[...] = to_trans[SLOTS - 1 :, :]
        watch_s[...], fixed_s[...] = next_watch_s[...], next_fixed_s[...]
        next_watch_s[...], next_fixed_s[...] = new_watch, new_fixed
        carry_s[...], cross_s[...], noise_s[...] = linked

        @pl.when(inside)
        def _():
            counted = jnp.minimum(taken, off_s[0, step + 1] - first)
            logs = jnp.where(iota((SLOTS, size), 0) < counted, jnp.log(pivots), 0.0)
            log_det = jnp.sum(logs, axis=0, keepdims=True)
            squares = jnp.where(iota((1, size), 1) < counted, quad, 0.0)
            squares = jnp.sum(squares, axis=1, keepdims=True)
            count = counted.astype(F32) * LOG_TWO_PI
            kept_lik[mine] = kept_lik[mine] + (log_det + squares + count)

        return state[4:] + after_next

    lax.while_loop(lambda state: state[0] < steps, body, opening + second)

    info, pull = info_s[...], pull_s[...]
    for j in range(own - 1, -1, -1):
        cov = kept_cov[j]
        smooth_cov_ref[j] = cov - dot(dot(cov, info), cov)
        smooth_mean_ref[j : j + 1, :] = kept_mean[j] + dot(pull, cov)
        loglik_ref[:, j : j + 1] = kept_lik[j][:, :1] * (-1.0 / (2.0 * size))
        if j > 0:
            trans = kept_trans[j]
            info = kept_info[j] + dot(dot(trans, info, TN), trans)
            pull = kept_pull[j] + dot(pull, trans)


VMEM = pl.BlockSpec(memory_space=pltpu.VMEM)
LIMIT = 48 * 1024 * 1024


def tables(nw, damping, process_var, obs_var, prior_mean, prior_var):
    size = nw.shape[1]
    return pl.pallas_call(
        tables_kernel,
        out_shape=(
            jax.ShapeDtypeStruct((size, 2 * WINDOW * 3 * size), BF),
            jax.ShapeDtypeStruct((2 * size, (WINDOW - 1) * size), BF),
            jax.ShapeDtypeStruct((WINDOW + 1, size, size), F32),
            jax.ShapeDtypeStruct((8, size), F32),
        ),
        in_specs=[VMEM] * 6,
        out_specs=(VMEM,) * 4,
        compiler_params=pltpu.CompilerParams(vmem_limit_bytes=LIMIT),
        cost_estimate=pl.CostEstimate(flops=10**8, bytes_accessed=2 * 10**6, transcendentals=0),
    )(nw, damping, process_var, obs_var, prior_mean, prior_var)


def chain(position, gathered, strip, big, added, line, own):
    steps, size = gathered.shape[0], gathered.shape[1] // 2
    padded = -(-(steps + WINDOW + 1) // 128) * 128
    square = (size, size)
    return pl.pallas_call(
        functools.partial(chain_kernel, own),
        out_shape=(
            jax.ShapeDtypeStruct((own, size), F32),
            jax.ShapeDtypeStruct((own, size, size), F32),
            jax.ShapeDtypeStruct((1, own), F32),
        ),
        in_specs=[pl.BlockSpec(memory_space=pltpu.SMEM)] + [VMEM] * 5,
        out_specs=(VMEM,) * 3,
        scratch_shapes=[
            pltpu.VMEM((padded, size), F32),
            pltpu.VMEM((padded, size), F32),
            pltpu.VMEM((padded, size), jnp.int32),
            pltpu.VMEM((8, padded), jnp.int32),
            pltpu.SMEM((8, padded), jnp.int32),
            pltpu.VMEM((SLOTS, 3 * size), BF),
            pltpu.VMEM((SLOTS, size), F32),
            pltpu.VMEM((SLOTS, SLOTS), F32),
            pltpu.VMEM((SLOTS, 3 * size), BF),
            pltpu.VMEM((SLOTS, SLOTS), F32),
            pltpu.VMEM((SLOTS, SLOTS), F32),
            pltpu.VMEM((SLOTS, 3 * size), BF),
            pltpu.VMEM((SLOTS, size), F32),
            pltpu.VMEM(square, F32),
            pltpu.VMEM(square, F32),
            pltpu.VMEM(square, F32),
            pltpu.VMEM((1, size), F32),
            pltpu.VMEM((1, size), F32),
            pltpu.VMEM((own,) + square, F32),
            pltpu.VMEM((own, 1, size), F32),
            pltpu.VMEM((own,) + square, F32),
            pltpu.VMEM((own,) + square, F32),
            pltpu.VMEM((own, 1, size), F32),
            pltpu.VMEM((own, 1, size), F32),
            pltpu.SemaphoreType.DMA(()),
        ],
        compiler_params=pltpu.CompilerParams(vmem_limit_bytes=LIMIT),
    )(position, gathered, strip, big, added, line)


def gather_all(observed, obs_mask, axis):
    size = lax.axis_size(axis)

    def joined(*pieces):
        masks = [mask.astype(F32) for mask in pieces[1::2]]
        return jnp.concatenate(
            [jnp.concatenate(pieces[::2], axis=0), jnp.concatenate(masks, axis=0)], axis=1
        )

    def across(array, reach):
        return lax.ppermute(array, axis, [(i, i ^ reach) for i in range(size)])

    if size == 1 or size & (size - 1):
        return lax.all_gather(joined(observed, obs_mask), axis, tiled=True), jnp.int32(0)
    held = joined(observed, obs_mask, across(observed, 1), across(obs_mask, 1))
    reach = 2
    while reach < size:
        held = jnp.concatenate([held, across(held, reach)], axis=0)
        reach *= 2
    return held, lax.axis_index(axis).astype(jnp.int32)


def local(
    observed, obs_mask, prior_mean, prior_var, neighbor_weights, damping, process_var, obs_var
):
    own = observed.shape[0]
    gathered, flip = gather_all(observed, obs_mask, "tm")
    position = jnp.stack([lax.axis_index("tm").astype(jnp.int32), flip])
    made = tables(
        neighbor_weights, damping[None], process_var[None], obs_var[None], prior_mean[None], prior_var[None]
    )
    smooth_mean, smooth_cov, loglik = chain(position, gathered, *made, own)
    return smooth_mean, smooth_cov, loglik.reshape(own)


def solution(mesh):
    return jax.shard_map(
        local,
        mesh=mesh,
        in_specs=(
            P(("parts", "tm"), None),
            P(("parts", "tm"), None),
            P("parts"),
            P("parts"),
            P(),
            P(),
            P(),
            P(),
        ),
        out_specs=(P(("parts", "tm"), None), P(("parts", "tm"), None, None), P(("parts", "tm"))),
        check_vma=False,
    )
```
